32 devices in a mesh: row: 8 (over z, x), col: 4 (over y, core).
Axes of the slice: x: 2, y: 2, z: 4, core: 2. Of those that a mesh axis runs over, the one named last changes fastest.
Arguments:
- features: bfloat16 [16384, 128], P(('col', 'row')), may hold values from -6 to 6
- weight: bfloat16 [128, 128], replicated, may hold values from -0.5 to 0.5
- bias_terms: float32 [128], replicated, may hold values from -3 to 3
- blocks: bfloat16 [640, 512, 128], P('row', 'col'), may hold values from -0.15625 to 0.15625
- block_rows: int32 [640, 4], P('row', 'col'), may hold values from 0 to 15, as said below
- block_cols: int32 [640, 4], P('row', 'col'), may hold values from 0 to 31, as said below
- tile_slot_count: int32 [8, 4], P('row', 'col'), may hold values from 10 to 80, as said below
- cotangent: bfloat16 [16384, 128], P(('row', 'col')), may hold values from -6 to 6
Outputs:
- hidden_out: bfloat16 [16384, 128], P(('row', 'col'))
- feat_grad: float32 [16384, 128], P(('col', 'row'))
- weight_grad: float32 [128, 128], replicated
- bias_grad: float32 [128], replicated
The draws below stay inside these ranges and needn't reach their ends.
Inputs may be any that keep to these rules, and one draw needn't show every extreme that they name: `block_rows`: only the first tile_slot_count slots of a tile are live; the live slots of one tile name distinct pairs of row block and column block. `block_cols`: column block of each slot, paired with block_rows. `tile_slot_count`: some tile has all 80 slots live.
All inputs are finite; a program needn't handle non-finite values.
Results may differ from the reference program's by a relative error of at most 0.019.
Values may be sent and summed in bfloat16 or wider, within the bound.
No kernel may reach another device: no remote copies, remote signals or barrier semaphores. Data moves between devices by JAX's collectives and lax.ppermute only.
A program may use at most 64 MiB of HBM per device.

```python
import math
from functools import partial
import jax
import jax.numpy as jnp
from jax import lax

F = 128
HID = 128
BS = 128
ROWS_DEV = 512
KMAX = 80
NODES = 16384
TILE_ROWB = 16
TILE_COLB = 32
N_ROW = 8
N_COL = 4


def slot_pairs(key):
    subkeys = jax.random.split(jax.random.fold_in(key, 11), N_ROW * N_COL)
    chosen = jax.vmap(lambda subkey: jax.random.permutation(subkey, TILE_ROWB * TILE_COLB)[:KMAX])(subkeys)
    chosen = chosen.reshape(N_ROW, N_COL, KMAX).transpose(0, 2, 1).reshape(N_ROW * KMAX, N_COL)
    return chosen.astype(jnp.int32)


def draw_block_rows(key, part):
    return (slot_pairs(key) // TILE_COLB).astype(jnp.int32)


def draw_block_cols(key, part):
    return (slot_pairs(key) % TILE_COLB).astype(jnp.int32)


def draw_tile_slot_count(key, part):
    levels = jax.random.randint(jax.random.fold_in(key, 23), (N_ROW * N_COL,), 0, 4).astype(jnp.int32)
    counts_flat = jnp.right_shift(jnp.int32(KMAX), levels)
    chosen_tile = jax.random.randint(jax.random.fold_in(key, 29), (), 0, N_ROW * N_COL).astype(jnp.int32)
    counts_flat = jnp.where(jnp.arange(N_ROW * N_COL, dtype=jnp.int32) == chosen_tile, jnp.int32(KMAX), counts_flat)
    return counts_flat.reshape(N_ROW, N_COL).astype(jnp.int32)


def steps_of(own_key, shape, cuts, low, largest):
    def one(position, blocks):
        draws = jax.random.uniform(jax.random.fold_in(jax.random.fold_in(own_key, 6), position), (blocks,), jnp.float32, low / len(cuts), largest / len(cuts))
        return jnp.repeat(jnp.exp(draws), shape[position] // blocks).reshape((-1,) + (1,) * (len(shape) - position - 1))

    level = one(*cuts[0])
    for cut in cuts[1:]:
        level = level * one(*cut)
    return level


def noise(key, shape, scale, most, shards=(), kind=jnp.bfloat16):
    level = steps_of(key, shape, shards, -0.22, 0.18) if shards else 1.0
    drawn = jax.random.normal(key, shape, jnp.float32) * scale * level
    return jnp.minimum(jnp.maximum(drawn, -most), most).astype(kind)


def setup_inputs(seed: int = 0) -> dict:
    splits = jax.random.split(jax.random.key(seed), 9)
    features = noise(splits[0], (NODES, F), 1.0, 6.0, ((0, 32),))
    weight = noise(splits[1], (F, HID), F ** -0.5, 0.5)
    bias_terms = noise(splits[2], (HID,), 0.5, 3.0, (), jnp.float32)
    blocks = noise(splits[3], (N_ROW * KMAX, N_COL * BS, BS), (KMAX * BS * BS // (2 * ROWS_DEV)) ** -0.5, 0.15625, ((0, 8), (1, 4)))
    block_rows = draw_block_rows(jax.random.fold_in(splits[8], 71), 0)
    block_cols = draw_block_cols(jax.random.fold_in(splits[8], 71), 0)
    tile_slot_count = draw_tile_slot_count(jax.random.fold_in(splits[8], 71), 0)
    cotangent = noise(splits[7], (NODES, HID), 1.0, 6.0, ((0, 32),))
    return {"features": features, "weight": weight, "bias_terms": bias_terms, "blocks": blocks, "block_rows": block_rows, "block_cols": block_cols, "tile_slot_count": tile_slot_count, "cotangent": cotangent}


def per_tile_forward(local_block_list, row_index_list, column_index_list, active_slot_count, source_features, row_block_index, column_block_index):
    channels = source_features.shape[1]
    active_flags = (jnp.arange(local_block_list.shape[0], dtype=jnp.int32) < active_slot_count).astype(jnp.float32)
    picked = source_features.reshape(column_block_index, BS, channels)[column_index_list]
    block_product = jnp.einsum('kab,kbf->kaf', local_block_list.astype(jnp.float32), picked.astype(jnp.float32))
    block_product = block_product * active_flags[:, None, None]
    return jax.ops.segment_sum(block_product, row_index_list, num_segments=row_block_index).reshape(row_block_index * BS, channels)

def per_tile_backward(local_block_list, row_index_list, column_index_list, active_slot_count, source_features, row_block_index, column_block_index):
    channels = source_features.shape[1]
    active_flags = (jnp.arange(local_block_list.shape[0], dtype=jnp.int32) < active_slot_count).astype(jnp.float32)
    picked = source_features.reshape(row_block_index, BS, channels)[row_index_list]
    block_product = jnp.einsum('kab,kaf->kbf', local_block_list.astype(jnp.float32), picked.astype(jnp.float32))
    block_product = block_product * active_flags[:, None, None]
    return jax.ops.segment_sum(block_product, column_index_list, num_segments=column_block_index).reshape(column_block_index * BS, channels)

def reference(features, weight, bias_terms, blocks, block_rows, block_cols, tile_slot_count, cotangent):
    row_block_index = TILE_ROWB
    column_block_index = TILE_COLB
    tile_height = row_block_index * BS
    tile_width = column_block_index * BS

    def slot_data(step):
        step = step.astype(jnp.int32)
        row_at = step // N_COL
        col_at = step % N_COL
        zero_index = jnp.int32(0)
        local_block_list = lax.dynamic_slice(blocks, (row_at * KMAX, col_at * BS, zero_index), (KMAX, BS, BS))
        row_index_list = lax.dynamic_slice(block_rows, (row_at * KMAX, col_at), (KMAX, 1))[:, 0]
        column_index_list = lax.dynamic_slice(block_cols, (row_at * KMAX, col_at), (KMAX, 1))[:, 0]
        active_slot_count = lax.dynamic_slice(tile_slot_count, (row_at, col_at), (1, 1))[0, 0]
        return (row_at, col_at, local_block_list, row_index_list, column_index_list, active_slot_count)

    def forward_step(step, totals):
        row_at, col_at, local_block_list, row_index_list, column_index_list, active_slot_count = slot_data(step)
        source_features = lax.dynamic_slice_in_dim(features, col_at * tile_width, tile_width, 0)
        partial_sum = per_tile_forward(local_block_list, row_index_list, column_index_list, active_slot_count, source_features, row_block_index, column_block_index)
        current = lax.dynamic_slice_in_dim(totals, row_at * tile_height, tile_height, 0)
        return lax.dynamic_update_slice_in_dim(totals, current + partial_sum, row_at * tile_height, 0)
    aggregate = lax.fori_loop(0, N_ROW * N_COL, forward_step, jnp.zeros((NODES, F), jnp.float32))
    aggregate_b = aggregate.astype(jnp.bfloat16)
    preact = jnp.dot(aggregate_b, weight, preferred_element_type=jnp.float32) + bias_terms.astype(jnp.float32)
    hidden, pullback = jax.vjp(partial(jax.nn.gelu, approximate=True), preact)
    dpreact = pullback(cotangent.astype(jnp.float32))[0]
    dpreact_b = dpreact.astype(jnp.bfloat16)
    scaling = 1.0 / math.sqrt(NODES)
    weight_grad = jnp.dot(aggregate_b.T, dpreact_b, preferred_element_type=jnp.float32) * scaling
    bias_grad = lax.optimization_barrier(jnp.sum(dpreact, axis=0)) * scaling
    back = jnp.dot(dpreact_b, weight.T, preferred_element_type=jnp.float32).astype(jnp.bfloat16)

    def backward_step(step, totals):
        row_at, col_at, local_block_list, row_index_list, column_index_list, active_slot_count = slot_data(step)
        source_features = lax.dynamic_slice_in_dim(back, row_at * tile_height, tile_height, 0)
        partial_sum = per_tile_backward(local_block_list, row_index_list, column_index_list, active_slot_count, source_features, row_block_index, column_block_index)
        current = lax.dynamic_slice_in_dim(totals, col_at * tile_width, tile_width, 0)
        return lax.dynamic_update_slice_in_dim(totals, current + partial_sum, col_at * tile_width, 0)
    feat_grad = lax.fori_loop(0, N_ROW * N_COL, backward_step, jnp.zeros((NODES, F), jnp.float32))
    return (hidden.astype(jnp.bfloat16), feat_grad, weight_grad, bias_grad)
```

```python
from functools import partial
import math

import jax
import jax.numpy as jnp
from jax import lax
from jax.experimental import pallas as pl
from jax.experimental.pallas import tpu as pltpu
from jax.sharding import PartitionSpec as P

BS = 128
C0 = 0.7978845608
C1 = 0.044715
ANY = pl.BlockSpec(memory_space=pl.ANY)
SMEM = pl.BlockSpec(memory_space=pltpu.SMEM)
VMEM = pl.BlockSpec(memory_space=pltpu.VMEM)


def mirror_masks(size):
    masks = []
    while size > 1:
        masks.append(size - 1)
        size //= 2
    return masks


def steps_to(offset, masks):
    steps = []
    for mask in masks:
        if offset & ((mask + 1) >> 1):
            steps.append(mask)
            offset ^= mask
    return steps


def tree(outer, inner, shortcut):
    assert outer & (outer - 1) == 0 and inner & (inner - 1) == 0
    outer_masks, inner_masks = mirror_masks(outer), mirror_masks(inner)
    found = []
    for o in range(outer):
        o_steps = steps_to(o, outer_masks)
        for i in range(inner):
            i_steps = steps_to(i, inner_masks)
            if o == 0 and i == 0:
                continue
            if i and not (shortcut and o == 1):
                parent = (o, i ^ i_steps[-1])
            else:
                parent = (o ^ o_steps[-1], i)
            depth = len(o_steps) + len(i_steps)
            found.append((depth, o * inner + i, parent[0] * inner + parent[1]))
    found.sort()
    return [(offset, parent) for _, offset, parent in found]


def row_tree(size):
    inner = 1
    while 2 * (2 * inner) * (2 * inner) <= size:
        inner *= 2
    return tree(size // inner, inner, True)


def col_tree(size):
    return tree(size // 2, 2, False)


def swap(x, axis, mask):
    size = lax.axis_size(axis)
    return lax.ppermute(x, axis, [(i, i ^ mask) for i in range(size)])


def spread(x, axis, routes):
    pieces = {0: x}
    for offset, parent in routes:
        pieces[offset] = swap(pieces[parent], axis, offset ^ parent)
    return [pieces[d] for d in range(len(pieces))]


def collect(pieces, axis, routes):
    terms = {d: [p] for d, p in enumerate(pieces)}
    for offset, parent in reversed(routes):
        total = terms[offset][0].astype(jnp.float32)
        for other in terms[offset][1:]:
            total = total + other.astype(jnp.float32)
        terms[parent].append(swap(total.astype(jnp.bfloat16), axis, offset ^ parent))
    return terms[0]


def unroll_of(slots):
    for u in (8, 4, 2):
        if slots % u == 0:
            return u
    return 1


def sparse_kernel(slots, count, per, transposed, idx, blocks, *refs):
    pieces, refs = refs[:count], refs[count:]
    outs, (held, source, total, piece_sem, block_sem) = refs[:-5], refs[-5:]
    here, there = idx[2 * slots + 1], idx[2 * slots + 2]
    live = idx[2 * slots]
    unroll = unroll_of(slots)
    copies = []
    for d in range(count):
        at = pl.multiple_of(lax.bitwise_xor(here, d) * per, per)
        copies.append(
            pltpu.make_async_copy(pieces[d], source.at[pl.ds(at, per)], piece_sem.at[d])
        )
    block_copy = pltpu.make_async_copy(blocks, held, block_sem)
    block_copy.start()
    for copy in copies:
        copy.start()
    sinks = total.shape[0] - 1
    total[...] = jnp.zeros_like(total)
    for copy in copies:
        copy.wait()
    block_copy.wait()

    def step(i, carry):
        products, targets = [], []
        for u in range(unroll):
            k = i * unroll + u
            row, col = idx[k], idx[slots + k]
            if transposed:
                products.append(
                    jnp.dot(source[row], held[k], preferred_element_type=jnp.float32)
                )
                target = col
            else:
                products.append(
                    jnp.dot(held[k], source[col], preferred_element_type=jnp.float32)
                )
                target = row
            targets.append(jnp.where(k < live, target, sinks))
        for product, target in zip(products, targets):
            total[target] = total[target] + product
        return carry

    lax.fori_loop(0, lax.div(live + unroll - 1, unroll), step, 0)
    for d, out in enumerate(outs):
        at = lax.bitwise_xor(there, d) * out.shape[0]
        out[...] = total[pl.ds(at, out.shape[0])].astype(out.dtype)


def sparse(idx, blocks, pieces, out_count, targets, transposed):
    slots = blocks.shape[0]
    count, per = len(pieces), pieces[0].shape[0]
    out_per = targets // out_count
    block = blocks.shape[1:]
    out_shape = [
        jax.ShapeDtypeStruct((out_per,) + block, jnp.float32 if d == 0 else jnp.bfloat16)
        for d in range(out_count)
    ]
    flops = 2 * slots * BS * BS * BS
    size = 2 * BS * BS
    need = size * (slots + count * per + 2 * (targets + 1) + targets + out_per) + (4 << 20)
    return pl.pallas_call(
        partial(sparse_kernel, slots, count, per, transposed),
        out_shape=out_shape,
        in_specs=[SMEM, ANY] + [ANY] * count,
        out_specs=[VMEM] * out_count,
        scratch_shapes=[
            pltpu.VMEM(blocks.shape, blocks.dtype),
            pltpu.VMEM((count * per,) + block, jnp.bfloat16),
            pltpu.VMEM((targets + 1,) + block, jnp.float32),
            pltpu.SemaphoreType.DMA((count,)),
            pltpu.SemaphoreType.DMA,
        ],
        compiler_params=pltpu.CompilerParams(vmem_limit_bytes=need),
        cost_estimate=pl.CostEstimate(
            flops=flops, bytes_accessed=size * (slots + count * per), transcendentals=0
        ),
    )(idx, blocks, *pieces)


def dense_kernel(scaling, terms, *refs):
    parts, refs = refs[:terms], refs[terms:]
    weight, bias, cotangent, hidden, back, weight_terms, bias_terms = refs
    rows = cotangent.shape[0]
    aggregate = parts[0][...].astype(jnp.float32)
    for part in parts[1:]:
        aggregate = aggregate + part[...].astype(jnp.float32)
    aggregate_b = aggregate.astype(jnp.bfloat16).reshape(rows, aggregate.shape[-1])
    v = jnp.dot(aggregate_b, weight[...], preferred_element_type=jnp.float32) + bias[...]
    square = v * v
    t = jnp.tanh(C0 * (v + C1 * (v * square)))
    half = 0.5 * (1.0 + t)
    hidden[...] = (v * half).astype(jnp.bfloat16)
    slope = half + (0.5 * v) * (1.0 - t * t) * (C0 * (1.0 + (3.0 * C1) * square))
    dpreact = cotangent[...].astype(jnp.float32) * slope
    dpreact_b = dpreact.astype(jnp.bfloat16)
    for n in range(rows // BS):
        back[n] = lax.dot_general(
            weight[...],
            dpreact_b[n * BS : (n + 1) * BS],
            (((1,), (1,)), ((), ())),
            preferred_element_type=jnp.float32,
        ).astype(jnp.bfloat16)
    weight_terms[...] = scaling * lax.dot_general(
        aggregate_b, dpreact_b, (((0,), (0,)), ((), ())), preferred_element_type=jnp.float32
    )
    bias_terms[...] = jnp.broadcast_to(
        scaling * jnp.sum(dpreact, axis=0, keepdims=True), bias_terms.shape
    )


def dense(parts, weight, bias, cotangent, scaling):
    rows, channels = cotangent.shape[0], weight.shape[0]
    return pl.pallas_call(
        partial(dense_kernel, scaling, len(parts)),
        out_shape=[
            jax.ShapeDtypeStruct(cotangent.shape, jnp.bfloat16),
            jax.ShapeDtypeStruct((rows // BS, channels, BS), jnp.bfloat16),
            jax.ShapeDtypeStruct(weight.shape, jnp.float32),
            jax.ShapeDtypeStruct((8, weight.shape[1]), jnp.float32),
        ],
        in_specs=[VMEM] * (len(parts) + 3),
        out_specs=[VMEM] * 4,
        compiler_params=pltpu.CompilerParams(vmem_limit_bytes=24 << 20),
        cost_estimate=pl.CostEstimate(
            flops=6 * rows * BS * BS, bytes_accessed=1 << 20, transcendentals=rows * BS
        ),
    )(*parts, weight, bias, cotangent)


def finish_kernel(*refs):
    parts, out = refs[:-1], refs[-1]
    for n in range(parts[0].shape[0]):
        total = parts[0][n].astype(jnp.float32)
        for part in parts[1:]:
            total = total + part[n].astype(jnp.float32)
        out[n * BS : (n + 1) * BS] = total.T


def finish(parts):
    per, channels, nodes = parts[0].shape
    return pl.pallas_call(
        finish_kernel,
        out_shape=jax.ShapeDtypeStruct((per * nodes, channels), jnp.float32),
        in_specs=[VMEM] * len(parts),
        out_specs=VMEM,
        compiler_params=pltpu.CompilerParams(vmem_limit_bytes=16 << 20),
    )(*parts)


def on_device(
    features, weight, bias_terms, blocks, block_rows, block_cols, tile_slot_count, cotangent
):
    own_rows, channels = features.shape
    row_devices, col_devices = lax.axis_size("row"), lax.axis_size("col")
    own_blocks = own_rows // BS
    row_blocks, column_blocks = own_blocks * col_devices, own_blocks * row_devices
    on_row, on_col = row_tree(row_devices), col_tree(col_devices)
    row_at = lax.axis_index("row").astype(jnp.int32)
    col_at = lax.axis_index("col").astype(jnp.int32)
    slots = jnp.concatenate([block_rows[:, 0], block_cols[:, 0], tile_slot_count[0]])
    idx_forward = jnp.concatenate([slots, jnp.stack([row_at, col_at])])
    idx_backward = jnp.concatenate([slots, jnp.stack([col_at, row_at])])

    own = features.reshape(own_blocks, BS, channels)
    columns = spread(own, "row", on_row)
    partial_sums = sparse(idx_forward, blocks, columns, col_devices, row_blocks, False)
    parts = collect(partial_sums, "col", on_col)

    scaling = 1.0 / math.sqrt(own_rows * row_devices * col_devices)
    hidden, back, weight_part, bias_part = dense(
        parts, weight, bias_terms.reshape(1, -1), cotangent, scaling
    )
    rows = spread(back, "col", on_col)
    gradient_sums = sparse(idx_backward, blocks, rows, row_devices, column_blocks, True)
    feat_grad = finish(collect(gradient_sums, "row", on_row))

    grads = jnp.concatenate([weight_part, bias_part], axis=0)
    for axis, masks in (("col", col_devices), ("row", row_devices)):
        mask = 1
        while mask < masks:
            grads = grads + swap(grads, axis, mask)
            mask *= 2
    return hidden, feat_grad, grads[:channels], grads[channels]


def solution(mesh):
    return jax.shard_map(
        on_device,
        mesh=mesh,
        in_specs=(
            P(("col", "row"), None),
            P(),
            P(),
            P("row", "col", None),
            P("row", "col"),
            P("row", "col"),
            P("row", "col"),
            P(("row", "col"), None),
        ),
        out_specs=(P(("row", "col"), None), P(("col", "row"), None), P(), P()),
        check_vma=False,
    )
```

```python
from functools import partial
import math

import jax
import jax.numpy as jnp
import numpy as np
from jax import lax
from jax.experimental import pallas as pl
from jax.experimental.pallas import tpu as pltpu
from jax.sharding import PartitionSpec as P

BS = 128
C0 = 0.7978845608
C1 = 0.044715
QUICK = pl.CostEstimate(flops=1, bytes_accessed=1, transcendentals=0)
ANY = pl.BlockSpec(memory_space=pl.ANY)
HBM = pl.BlockSpec(memory_space=pltpu.HBM)
SMEM = pl.BlockSpec(memory_space=pltpu.SMEM)
VMEM = pl.BlockSpec(memory_space=pltpu.VMEM)


def mirror_masks(size):
    masks = []
    while size > 1:
        masks.append(size - 1)
        size //= 2
    return masks


def steps_to(offset, masks):
    steps = []
    for mask in masks:
        if offset & ((mask + 1) >> 1):
            steps.append(mask)
            offset ^= mask
    return steps


def tree(outer, inner, shortcut):
    assert outer & (outer - 1) == 0 and inner & (inner - 1) == 0
    outer_masks, inner_masks = mirror_masks(outer), mirror_masks(inner)
    found = []
    for o in range(outer):
        o_steps = steps_to(o, outer_masks)
        for i in range(inner):
            i_steps = steps_to(i, inner_masks)
            if o == 0 and i == 0:
                continue
            short = bool(i) and shortcut and o == 1
            if i and not short:
                parent = (o, i ^ i_steps[-1])
            else:
                parent = (o ^ o_steps[-1], i)
            depth = len(o_steps) + len(i_steps)
            found.append((depth, short, -o, i, parent))
    found.sort()
    return [(-o * inner + i, parent[0] * inner + parent[1]) for _, _, o, i, parent in found]


def inner_of(size):
    inner = 1
    while 2 * (2 * inner) * (2 * inner) <= size:
        inner *= 2
    return inner


def depth_of(offset, routes):
    parents = dict(routes)
    depth = 0
    while offset:
        offset, depth = parents[offset], depth + 1
    return depth


def swap(x, axis, mask):
    size = lax.axis_size(axis)
    return lax.ppermute(x, axis, [(i, i ^ mask) for i in range(size)])


def after(x, *others):
    return lax.optimization_barrier((x,) + others)[0]


def spread(pieces, axis, routes):
    pieces = dict(pieces)
    for offset, parent in routes:
        pieces[offset] = swap(pieces[parent], axis, offset ^ parent)
    return pieces


def add(terms):
    total = terms[0].astype(jnp.float32)
    for other in terms[1:]:
        total = total + other.astype(jnp.float32)
    return total


def collect(pieces, axis, routes):
    terms = {d: [p] for d, p in pieces.items()}
    for offset, parent in reversed(routes):
        total = add(terms.pop(offset)).astype(jnp.bfloat16)
        terms[parent].append(swap(total, axis, offset ^ parent))
    return terms


def unroll_of(slots):
    for u in (8, 4, 2):
        if slots % u == 0:
            return u
    return 1


def member(offset, chosen):
    mask = np.uint32(sum(1 << d for d in chosen)).astype(np.int32)
    return lax.bitwise_and(lax.shift_right_logical(jnp.int32(mask), offset), 1)


FORWARD_EARLY, FORWARD_LATE, BACK_FIRST, BACK_LAST = range(4)
LENGTHS, ROW_AT, COL_AT = 0, 4, 5


def prep_kernel(
    per, late, first, in_rows, in_cols, in_live, blocks,
    table, held, rows, cols, live, sem, small_sem,
):
    slots = blocks.shape[0]
    copy = pltpu.make_async_copy(blocks, held, sem)
    copy.start()
    small = [
        pltpu.make_async_copy(source, target, small_sem.at[n])
        for n, (source, target) in enumerate(((in_rows, rows), (in_cols, cols), (in_live, live)))
    ]
    for one in small:
        one.start()
    for one in small:
        one.wait()
    row_at, col_at = lax.axis_index("row"), lax.axis_index("col")

    def step(k, lengths):
        row, col = rows[k], cols[k]
        table[k] = row
        table[slots + k] = col
        in_use = (k < live[0]).astype(jnp.int32)
        offset = lax.bitwise_xor(row_at, lax.div(col, per))
        is_late, is_first = member(offset, late), member(offset, first)
        flags = (1 - is_late, is_late, is_first, 1 - is_first)
        for n, length in enumerate(lengths):
            table[(2 + n) * slots + length] = k
        return tuple(length + flag * in_use for length, flag in zip(lengths, flags))

    lengths = lax.fori_loop(0, slots, step, (jnp.int32(0),) * 4)
    for n, length in enumerate(lengths):
        table[6 * slots + n] = length
    table[6 * slots + ROW_AT] = row_at
    table[6 * slots + COL_AT] = col_at
    copy.wait()


def prep(block_rows, block_cols, tile_slot_count, blocks, per, late, first):
    slots = blocks.shape[0]
    return pl.pallas_call(
        partial(prep_kernel, per, late, first),
        out_shape=[
            jax.ShapeDtypeStruct((6 * slots + 8,), jnp.int32),
            jax.ShapeDtypeStruct(blocks.shape, blocks.dtype),
        ],
        in_specs=[HBM] * 4,
        out_specs=[SMEM, VMEM],
        scratch_shapes=[
            pltpu.SMEM((slots,), jnp.int32),
            pltpu.SMEM((slots,), jnp.int32),
            pltpu.SMEM((1,), jnp.int32),
            pltpu.SemaphoreType.DMA,
            pltpu.SemaphoreType.DMA((3,)),
        ],
        compiler_params=pltpu.CompilerParams(vmem_limit_bytes=50 << 20),
        cost_estimate=QUICK,
    )(block_rows.reshape(slots), block_cols.reshape(slots), tile_slot_count.reshape(1), blocks)


def sparse_kernel(which, offsets, here, there, sums, starts, *refs):
    transposed = which >= BACK_FIRST
    table, held = refs[:2]
    pieces, refs = refs[2 : 2 + len(offsets)], refs[2 + len(offsets) :]
    before = None
    if starts:
        before, refs = refs[0], refs[1:]
    if sums is None:
        total, source, sem = refs
    else:
        outs, (source, total, sem) = refs[: len(sums)], refs[len(sums) :]
    slots = held.shape[0]
    unroll = unroll_of(slots)
    per = pieces[0].shape[0]
    copies = []
    for n, offset in enumerate(offsets):
        at = lax.bitwise_xor(table[6 * slots + here], offset) * per
        copies.append(
            pltpu.make_async_copy(pieces[n], source.at[pl.ds(at, per)], sem.at[n])
        )
        copies[-1].start()
    places = []
    if sums is not None:
        out_per = outs[0].shape[0]
        places = [
            pl.ds(lax.bitwise_xor(table[6 * slots + there], d) * out_per, out_per) for d in sums
        ]
    if starts:
        for place in places:
            total[place] = before[place]
    elif places:
        for place, out in zip(places, outs):
            total[place] = jnp.zeros(out.shape, jnp.float32)
    else:
        total[...] = jnp.zeros_like(total)
    sink = total.shape[0] - 1
    length = table[6 * slots + which]
    for copy in copies:
        copy.wait()

    def step(i, carry):
        products, targets = [], []
        for u in range(unroll):
            n = i * unroll + u
            in_use = n < length
            k = jnp.where(in_use, table[(2 + which) * slots + n], 0)
            row, col = table[k], table[slots + k]
            if transposed:
                row = jnp.where(in_use, row, lax.bitwise_xor(table[6 * slots + here], offsets[0]) * per)
                products.append(
                    jnp.dot(source[row], held[k], preferred_element_type=jnp.float32)
                )
                target = col
            else:
                col = jnp.where(in_use, col, lax.bitwise_xor(table[6 * slots + here], offsets[0]) * per)
                products.append(
                    jnp.dot(held[k], source[col], preferred_element_type=jnp.float32)
                )
                target = row
            targets.append(jnp.where(in_use, target, sink))
        for product, target in zip(products, targets):
            total[target] = total[target] + product
        return carry

    lax.fori_loop(0, lax.div(length + unroll - 1, unroll), step, 0)
    if sums is not None:
        for out, place in zip(outs, places):
            out[...] = total[place].astype(out.dtype)


def sparse(which, table, held, pieces, here, there, sources, targets, before=None, sums=None, out_per=0):
    offsets = sorted(pieces)
    per = pieces[offsets[0]].shape[0]
    block = held.shape[1:]
    whole = jax.ShapeDtypeStruct((targets + 1,) + block, jnp.float32)
    scratch = [
        pltpu.VMEM((sources,) + block, jnp.bfloat16),
        pltpu.VMEM(whole.shape, whole.dtype),
        pltpu.SemaphoreType.DMA((len(offsets),)),
    ]
    if sums is None:
        out_shape = whole
        scratch.pop(1)
    else:
        out_shape = [jax.ShapeDtypeStruct((out_per,) + block, sums[d]) for d in sums]
    operands = [table, held] + [pieces[d] for d in offsets]
    in_specs = [SMEM, VMEM] + [ANY] * len(offsets)
    if before is not None:
        operands.append(before)
        in_specs.append(VMEM)
    size = 2 * BS * BS
    need = size * (held.shape[0] + 2 * sources + 5 * (targets + 1)) + (6 << 20)
    return pl.pallas_call(
        partial(
            sparse_kernel,
            which,
            tuple(offsets),
            here,
            there,
            None if sums is None else tuple(sums),
            before is not None,
        ),
        out_shape=out_shape,
        in_specs=in_specs,
        out_specs=jax.tree.map(lambda _: VMEM, out_shape),
        scratch_shapes=scratch,
        compiler_params=pltpu.CompilerParams(vmem_limit_bytes=need),
        cost_estimate=QUICK,
    )(*operands)


def dense_kernel(scaling, count, weight, bias, *refs):
    parts = [refs[3 * n : 3 * n + 3] for n in range(count)]
    hidden, *backs, grads = refs[3 * count :]
    weight_grad = bias_grad = None
    for n, (mine, theirs, cotangent) in enumerate(parts):
        rows, channels = cotangent.shape[0], mine.shape[-1]
        aggregate = mine[...].astype(jnp.float32) + theirs[...].astype(jnp.float32)
        aggregate_b = aggregate.astype(jnp.bfloat16).reshape(rows, channels)
        v = jnp.dot(aggregate_b, weight[...], preferred_element_type=jnp.float32) + bias[...]
        square = v * v
        t = jnp.tanh(C0 * (v + C1 * (v * square)))
        half = 0.5 * (1.0 + t)
        if n == 0:
            hidden[...] = (v * half).astype(jnp.bfloat16)
        slope = half + (0.5 * v) * (1.0 - t * t) * (C0 * (1.0 + (3.0 * C1) * square))
        dpreact = cotangent[...].astype(jnp.float32) * slope
        dpreact_b = dpreact.astype(jnp.bfloat16)
        for m in range(rows // BS):
            backs[n][m] = lax.dot_general(
                weight[...],
                dpreact_b[m * BS : (m + 1) * BS],
                (((1,), (1,)), ((), ())),
                preferred_element_type=jnp.float32,
            ).astype(jnp.bfloat16)
        weight_part = scaling * lax.dot_general(
            aggregate_b, dpreact_b, (((0,), (0,)), ((), ())), preferred_element_type=jnp.float32
        )
        bias_part = scaling * jnp.sum(dpreact, axis=0, keepdims=True)
        if n == 0:
            weight_grad, bias_grad = weight_part, bias_part
        else:
            weight_grad, bias_grad = weight_grad + weight_part, bias_grad + bias_part
    channels = weight.shape[0]
    grads[:channels] = weight_grad
    grads[channels:] = jnp.broadcast_to(bias_grad, (grads.shape[0] - channels, bias_grad.shape[1]))


def dense(weight, bias, parts, scaling):
    cotangent = parts[0][2]
    rows, (channels, units) = cotangent.shape[0], weight.shape
    out_shape = [jax.ShapeDtypeStruct(cotangent.shape, jnp.bfloat16)]
    out_shape += [jax.ShapeDtypeStruct((rows // BS, channels, BS), jnp.bfloat16)] * len(parts)
    out_shape.append(jax.ShapeDtypeStruct((channels + 16, units), jnp.float32))
    operands = [weight, bias] + [x for part in parts for x in part]
    return pl.pallas_call(
        partial(dense_kernel, scaling, len(parts)),
        out_shape=out_shape,
        in_specs=[VMEM] * len(operands),
        out_specs=[VMEM] * len(out_shape),
        compiler_params=pltpu.CompilerParams(vmem_limit_bytes=32 << 20),
        cost_estimate=QUICK,
    )(*operands)


def finish_kernel(*refs):
    parts, out = refs[:-1], refs[-1]
    for n in range(parts[0].shape[0]):
        total = parts[0][n].astype(jnp.float32)
        for part in parts[1:]:
            total = total + part[n].astype(jnp.float32)
        out[n * BS : (n + 1) * BS] = total.T


def finish(parts):
    per, channels, nodes = parts[0].shape
    return pl.pallas_call(
        finish_kernel,
        out_shape=jax.ShapeDtypeStruct((per * nodes, channels), jnp.float32),
        in_specs=[VMEM] * len(parts),
        out_specs=VMEM,
        compiler_params=pltpu.CompilerParams(vmem_limit_bytes=16 << 20),
    )(*parts)


def on_device(
    features, weight, bias_terms, blocks, block_rows, block_cols, tile_slot_count, cotangent
):
    own_rows, channels = features.shape
    row_devices, col_devices = lax.axis_size("row"), lax.axis_size("col")
    per = own_rows // BS
    row_blocks, column_blocks = per * col_devices, per * row_devices
    inner = inner_of(row_devices)
    on_row = tree(row_devices // inner, inner, True)
    on_col = tree(col_devices // 2, 2, False)
    across = col_devices - 2
    on_col = [route for route in on_col if route[0] != across]
    late_columns = [d for d, _ in on_row[-(row_devices // 4) :]]
    parents = [parent for _, parent in on_row]
    first = [d for d, parent in on_row if parent and d not in parents]

    table, held = prep(
        block_rows, block_cols, tile_slot_count, blocks, per, late_columns, first
    )
    pieces = {0: features.reshape(per, BS, channels)}
    near = [route for route in on_row if not route[1]]
    far = [route for route in on_row if route[1]]
    top = near[0][0]
    second = [d for d, p in far if p == top and p ^ d >= inner][0]
    far.sort(key=lambda route: (depth_of(route[0], on_row), route[0] != second))
    pieces |= spread({0: pieces[0]}, "row", near[:1])
    pieces |= spread({0: after(pieces[0], table)}, "row", near[1:])
    pieces[top] = after(pieces[top], *(pieces[d] for d, _ in near[1:]))
    for offset, parent in far:
        source = pieces[parent]
        if parent in [d for d, _ in near[1:]]:
            source = after(source, pieces[second])
        pieces[offset] = swap(source, "row", offset ^ parent)
    other_cotangent = swap(after(cotangent, pieces[second]), "col", across)
    early = {d: p for d, p in pieces.items() if d not in late_columns}
    late = {d: p for d, p in pieces.items() if d in late_columns}
    late[late_columns[0]] = after(late[late_columns[0]], other_cotangent)
    total = sparse(FORWARD_EARLY, table, held, early, ROW_AT, COL_AT, column_blocks, row_blocks)
    sums = sparse(
        FORWARD_LATE, table, held, late, ROW_AT, COL_AT, column_blocks, row_blocks, total,
        {d: jnp.float32 if d in (0, across) else jnp.bfloat16 for d in range(col_devices)}, per,
    )

    terms = collect(dict(enumerate(sums)), "col", on_col)
    mine = add(terms[0]).astype(jnp.bfloat16)
    others = add(terms[across]).astype(jnp.bfloat16)
    to_mine, to_others = swap(others, "col", across), swap(mine, "col", across)
    scaling = 1.0 / math.sqrt(own_rows * row_devices * col_devices)
    bias = bias_terms.reshape(1, -1)
    hidden, back, other_back, grads = dense(
        weight, bias,
        [(mine, to_mine, cotangent), (others, to_others, other_cotangent)], scaling,
    )
    grads = grads + swap(grads, "col", 1)
    for mask in mirror_masks(col_devices // 2)[1:]:
        grads = grads + swap(grads, "col", 2 * mask)

    rows = spread({0: back, across: other_back}, "col", on_col)
    rows[0] = after(rows[0], grads)
    types = {d: jnp.bfloat16 if d else jnp.float32 for d in range(row_devices)}
    rest = [d for d in range(row_devices) if d not in first]
    leave_first, leave_last = [
        sparse(
            which, table, held, rows, COL_AT, ROW_AT, row_blocks, column_blocks,
            None, {d: types[d] for d in chosen}, per,
        )
        for which, chosen in ((BACK_FIRST, first), (BACK_LAST, rest))
    ]
    sums = dict(zip(first, leave_first)) | dict(zip(rest, leave_last))

    chain = [far[-1][0]]
    while chain[-1]:
        chain.append(dict(on_row)[chain[-1]])
    terms = {d: [p] for d, p in sums.items()}
    came, seen = {}, []
    for offset, parent in reversed(on_row):
        total = add(terms.pop(offset)).astype(jnp.bfloat16)
        mask = offset ^ parent
        if offset in chain:
            if mask not in seen:
                seen.append(mask)
                rounded = grads.astype(jnp.bfloat16)
                total, rounded = lax.optimization_barrier((total, rounded))
                grads = rounded.astype(jnp.float32) + swap(rounded, "row", mask).astype(jnp.float32)
        elif parent == 0:
            total = after(total, came[chain[0]])
        else:
            total = after(total, leave_last[0])
        came[offset] = swap(total, "row", mask)
        terms[parent].append(came[offset])
    for mask in mirror_masks(inner) + [inner * m for m in mirror_masks(row_devices // inner)]:
        if mask not in seen:
            rounded = grads.astype(jnp.bfloat16)
            grads = rounded.astype(jnp.float32) + swap(rounded, "row", mask).astype(jnp.float32)
    feat_grad = finish(terms[0])
    return hidden, feat_grad, grads[:channels], grads[channels]


def solution(mesh):
    return jax.shard_map(
        on_device,
        mesh=mesh,
        in_specs=(
            P(("col", "row"), None),
            P(),
            P(),
            P("row", "col", None),
            P("row", "col"),
            P("row", "col"),
            P("row", "col"),
            P(("row", "col"), None),
        ),
        out_specs=(P(("row", "col"), None), P(("col", "row"), None), P(), P()),
        check_vma=False,
    )
```

```python
from functools import partial
import math

import jax
import jax.numpy as jnp
import numpy as np
from jax import lax
from jax.experimental import pallas as pl
from jax.experimental.pallas import tpu as pltpu
from jax.sharding import PartitionSpec as P

BS = 128
C0 = 0.7978845608
C1 = 0.044715
QUICK = pl.CostEstimate(flops=1, bytes_accessed=1, transcendentals=0)
ANY = pl.BlockSpec(memory_space=pl.ANY)
HBM = pl.BlockSpec(memory_space=pltpu.HBM)
SMEM = pl.BlockSpec(memory_space=pltpu.SMEM)
VMEM = pl.BlockSpec(memory_space=pltpu.VMEM)


def mirror_masks(size):
    masks = []
    while size > 1:
        masks.append(size - 1)
        size //= 2
    return masks


def steps_to(offset, masks):
    steps = []
    for mask in masks:
        if offset & ((mask + 1) >> 1):
            steps.append(mask)
            offset ^= mask
    return steps


def tree(outer, inner, shortcut):
    assert outer & (outer - 1) == 0 and inner & (inner - 1) == 0
    outer_masks, inner_masks = mirror_masks(outer), mirror_masks(inner)
    found = []
    for o in range(outer):
        o_steps = steps_to(o, outer_masks)
        for i in range(inner):
            i_steps = steps_to(i, inner_masks)
            if o == 0 and i == 0:
                continue
            short = bool(i) and shortcut and o == 1
            if i and not short:
                parent = (o, i ^ i_steps[-1])
            else:
                parent = (o ^ o_steps[-1], i)
            depth = len(o_steps) + len(i_steps)
            found.append((depth, short, -o, i, parent))
    found.sort()
    return [(-o * inner + i, parent[0] * inner + parent[1]) for _, _, o, i, parent in found]


def inner_of(size):
    inner = 1
    while 2 * (2 * inner) * (2 * inner) <= size:
        inner *= 2
    return inner


def depth_of(offset, routes):
    parents = dict(routes)
    depth = 0
    while offset:
        offset, depth = parents[offset], depth + 1
    return depth


def swap(x, axis, mask, name="swap"):
    size = lax.axis_size(axis)
    with jax.named_scope(name):
        return lax.ppermute(x, axis, [(i, i ^ mask) for i in range(size)])


def after(x, *others):
    return lax.optimization_barrier((x,) + others)[0]


class Queue:
    def __init__(self):
        self.last = None

    def swap(self, x, axis, mask, name):
        if self.last is not None:
            x = after(x, self.last)
        self.last = x
        return swap(x, axis, mask, name)


def spread(pieces, axis, routes):
    pieces = dict(pieces)
    for offset, parent in routes:
        pieces[offset] = swap(pieces[parent], axis, offset ^ parent, f"rows_{offset}")
    return pieces


def add(terms):
    total = terms[0].astype(jnp.float32)
    for other in terms[1:]:
        total = total + other.astype(jnp.float32)
    return total


def collect(pieces, axis, routes):
    terms = {d: [p] for d, p in pieces.items()}
    for offset, parent in reversed(routes):
        total = add(terms.pop(offset)).astype(jnp.bfloat16)
        terms[parent].append(swap(total, axis, offset ^ parent, f"aggregate_{offset}"))
    return terms


def unroll_of(slots):
    for u in (8, 4, 2):
        if slots % u == 0:
            return u
    return 1


def member(offset, chosen):
    mask = np.uint32(sum(1 << d for d in chosen)).astype(np.int32)
    return lax.bitwise_and(lax.shift_right_logical(jnp.int32(mask), offset), 1)


FORWARD_EARLY, FORWARD_LATE, BACK_FIRST, BACK_LAST = range(4)


def widths(slots, row_blocks, column_blocks):
    bits = [(n - 1).bit_length() for n in (slots, row_blocks, column_blocks)]
    assert sum(bits) < 32
    return bits


def parts_of(slots):
    return 8 if slots % 8 == 0 else 1


def prep_kernel(per, bits, late, first, indices, blocks, table, held, sem):
    slots = blocks.shape[0]
    parts = parts_of(slots)
    copies = []
    for n in range(parts):
        place = pl.ds(n * (slots // parts), slots // parts)
        copies.append(pltpu.make_async_copy(blocks.at[place], held.at[place], sem.at[n]))
        copies[-1].start()
    row_at = lax.axis_index("row")
    live = indices[2 * slots]

    def step(i, lengths):
        early, late_ones, soon, last = lengths
        for u in range(unroll):
            k = i * unroll + u
            row, col = indices[k], indices[slots + k]
            entry = k + lax.shift_left(row, bits[0]) + lax.shift_left(col, bits[0] + bits[1])
            in_use = (k < live).astype(jnp.int32)
            offset = lax.bitwise_xor(row_at, lax.div(col, per))
            is_late, is_first = member(offset, late), member(offset, first)
            table[jnp.where(is_late == 1, slots - 1 - late_ones, early)] = entry
            table[slots + jnp.where(is_first == 1, soon, slots - 1 - last)] = entry
            early, late_ones = early + (1 - is_late) * in_use, late_ones + is_late * in_use
            soon, last = soon + is_first * in_use, last + (1 - is_first) * in_use
        return early, late_ones, soon, last

    unroll = 4 if slots % 4 == 0 else 1
    lengths = lax.fori_loop(0, lax.div(live + unroll - 1, unroll), step, (jnp.int32(0),) * 4)
    for n, length in enumerate(lengths):
        table[2 * slots + n] = length
    for copy in copies:
        copy.wait()


def prep(indices, blocks, per, bits, late, first):
    slots = blocks.shape[0]
    return pl.pallas_call(
        partial(prep_kernel, per, bits, late, first),
        out_shape=[
            jax.ShapeDtypeStruct((2 * slots + 8,), jnp.int32),
            jax.ShapeDtypeStruct(blocks.shape, blocks.dtype),
        ],
        in_specs=[SMEM, HBM],
        out_specs=[SMEM, VMEM],
        scratch_shapes=[pltpu.SemaphoreType.DMA((parts_of(slots),))],
        compiler_params=pltpu.CompilerParams(vmem_limit_bytes=50 << 20),
        cost_estimate=QUICK,
    )(indices, blocks)


def sparse_kernel(which, bits, offsets, here, there, sums, starts, *refs):
    transposed = which >= BACK_FIRST
    in_table, held = refs[:2]
    pieces, refs = refs[2 : 2 + len(offsets)], refs[2 + len(offsets) :]
    before = None
    if starts:
        before, refs = refs[0], refs[1:]
    if sums is None:
        total, table, source, sem = refs
    else:
        outs, (total, table, source, sem) = refs[: len(sums)], refs[len(sums) :]
    here, there = lax.axis_index(here), lax.axis_index(there)
    slots = held.shape[0]
    unroll = unroll_of(slots)
    per = pieces[0].shape[0]
    copies = [pltpu.make_async_copy(in_table, table, sem.at[len(offsets)])]
    copies[0].start()
    for n, offset in enumerate(offsets):
        at = lax.bitwise_xor(here, offset) * per
        copies.append(
            pltpu.make_async_copy(pieces[n], source.at[pl.ds(at, per)], sem.at[n])
        )
        copies[-1].start()
    places = []
    if sums is not None:
        out_per = outs[0].shape[0]
        places = [
            pl.ds(lax.bitwise_xor(there, d) * out_per, out_per) for d in sums
        ]
    if starts:
        for place in places:
            total[place] = before[place]
    elif places:
        for place, out in zip(places, outs):
            total[place] = jnp.zeros(out.shape, jnp.float32)
    else:
        total[...] = jnp.zeros_like(total)
    sink = total.shape[0] - 1
    for copy in copies:
        copy.wait()
    length = table[2 * slots + which]
    idle = lax.bitwise_xor(here, offsets[0]) * per

    def step(i, carry):
        products, targets = [], []
        for u in range(unroll):
            n = i * unroll + u
            in_use = n < length
            at = jnp.minimum(n, slots - 1)
            if which in (FORWARD_LATE, BACK_LAST):
                at = slots - 1 - at
            entry = jnp.where(in_use, table[slots * transposed + at], 0)
            k = lax.bitwise_and(entry, (1 << bits[0]) - 1)
            row = lax.bitwise_and(lax.shift_right_logical(entry, bits[0]), (1 << bits[1]) - 1)
            col = lax.shift_right_logical(entry, bits[0] + bits[1])
            if transposed:
                source_at, target = row, col
                lhs, rhs = source.at[jnp.where(in_use, source_at, idle)], held.at[k]
            else:
                source_at, target = col, row
                lhs, rhs = held.at[k], source.at[jnp.where(in_use, source_at, idle)]
            products.append(jnp.dot(lhs[...], rhs[...], preferred_element_type=jnp.float32))
            targets.append(jnp.where(in_use, target, sink))
        for product, target in zip(products, targets):
            total[target] = total[target] + product
        return carry

    lax.fori_loop(0, lax.div(length + unroll - 1, unroll), step, 0)
    if sums is not None:
        for out, place in zip(outs, places):
            out[...] = total[place].astype(out.dtype)


def sparse(which, bits, table, held, pieces, here, there, sources, targets, before=None, sums=None, out_per=0):
    offsets = sorted(pieces)
    per = pieces[offsets[0]].shape[0]
    block = held.shape[1:]
    whole = jax.ShapeDtypeStruct((targets + 1,) + block, jnp.float32)
    scratch = [
        pltpu.VMEM(whole.shape, whole.dtype),
        pltpu.SMEM(table.shape, table.dtype),
        pltpu.VMEM((sources,) + block, jnp.bfloat16),
        pltpu.SemaphoreType.DMA((len(offsets) + 1,)),
    ]
    if sums is None:
        out_shape = whole
        scratch.pop(0)
    else:
        out_shape = [jax.ShapeDtypeStruct((out_per,) + block, sums[d]) for d in sums]
    operands = [table, held] + [pieces[d] for d in offsets]
    in_specs = [ANY, VMEM] + [ANY] * len(offsets)
    if before is not None:
        operands.append(before)
        in_specs.append(VMEM)
    size = 2 * BS * BS
    need = size * (held.shape[0] + 2 * sources + 5 * (targets + 1)) + (6 << 20)
    return pl.pallas_call(
        partial(
            sparse_kernel,
            which,
            bits,
            tuple(offsets),
            here,
            there,
            None if sums is None else tuple(sums),
            before is not None,
        ),
        out_shape=out_shape,
        in_specs=in_specs,
        out_specs=jax.tree.map(lambda _: VMEM, out_shape),
        scratch_shapes=scratch,
        compiler_params=pltpu.CompilerParams(vmem_limit_bytes=need),
        cost_estimate=QUICK,
    )(*operands)


def dense_kernel(scaling, count, weight, bias, *refs):
    parts = [refs[3 * n : 3 * n + 3] for n in range(count)]
    hidden, *backs, grads = refs[3 * count :]
    weight_grad = bias_grad = None
    for n, (mine, theirs, cotangent) in enumerate(parts):
        rows, channels = cotangent.shape[0], mine.shape[-1]
        aggregate = mine[...].astype(jnp.float32) + theirs[...].astype(jnp.float32)
        aggregate_b = aggregate.astype(jnp.bfloat16).reshape(rows, channels)
        v = jnp.dot(aggregate_b, weight[...], preferred_element_type=jnp.float32) + bias[...]
        square = v * v
        t = jnp.tanh(C0 * (v + C1 * (v * square)))
        half = 0.5 * (1.0 + t)
        if n == 0:
            hidden[...] = (v * half).astype(jnp.bfloat16)
        slope = half + (0.5 * v) * (1.0 - t * t) * (C0 * (1.0 + (3.0 * C1) * square))
        dpreact = cotangent[...].astype(jnp.float32) * slope
        dpreact_b = dpreact.astype(jnp.bfloat16)
        for m in range(rows // BS):
            backs[n][m] = lax.dot_general(
                weight[...],
                dpreact_b[m * BS : (m + 1) * BS],
                (((1,), (1,)), ((), ())),
                preferred_element_type=jnp.float32,
            ).astype(jnp.bfloat16)
        weight_part = scaling * lax.dot_general(
            aggregate_b, dpreact_b, (((0,), (0,)), ((), ())), preferred_element_type=jnp.float32
        )
        bias_part = scaling * jnp.sum(dpreact, axis=0, keepdims=True)
        if n == 0:
            weight_grad, bias_grad = weight_part, bias_part
        else:
            weight_grad, bias_grad = weight_grad + weight_part, bias_grad + bias_part
    channels = weight.shape[0]
    grads[:channels] = weight_grad
    grads[channels:] = jnp.broadcast_to(bias_grad, (grads.shape[0] - channels, bias_grad.shape[1]))


def dense(weight, bias, parts, scaling):
    cotangent = parts[0][2]
    rows, (channels, units) = cotangent.shape[0], weight.shape
    out_shape = [jax.ShapeDtypeStruct(cotangent.shape, jnp.bfloat16)]
    out_shape += [jax.ShapeDtypeStruct((rows // BS, channels, BS), jnp.bfloat16)] * len(parts)
    out_shape.append(jax.ShapeDtypeStruct((channels + 16, units), jnp.float32))
    operands = [weight, bias] + [x for part in parts for x in part]
    return pl.pallas_call(
        partial(dense_kernel, scaling, len(parts)),
        out_shape=out_shape,
        in_specs=[VMEM] * len(operands),
        out_specs=[VMEM] * len(out_shape),
        compiler_params=pltpu.CompilerParams(vmem_limit_bytes=32 << 20),
        cost_estimate=QUICK,
    )(*operands)


def finish_kernel(*refs):
    mine, theirs = refs[:2]
    parts, (out, weight_grad, bias_grad) = refs[2:-3], refs[-3:]
    for n in range(parts[0].shape[0]):
        total = parts[0][n].astype(jnp.float32)
        for part in parts[1:]:
            total = total + part[n].astype(jnp.float32)
        out[n * BS : (n + 1) * BS] = total.T
    grads = mine[...].astype(jnp.float32) + theirs[...].astype(jnp.float32)
    channels = weight_grad.shape[0]
    weight_grad[...] = grads[:channels]
    bias_grad[...] = grads[channels : channels + 1]


def finish(parts, mine, theirs):
    per, channels, nodes = parts[0].shape
    units = mine.shape[1]
    out_shape = [
        jax.ShapeDtypeStruct(shape, jnp.float32)
        for shape in ((per * nodes, channels), (channels, units), (1, units))
    ]
    return pl.pallas_call(
        finish_kernel,
        out_shape=out_shape,
        in_specs=[VMEM] * (len(parts) + 2),
        out_specs=[VMEM] * 3,
        compiler_params=pltpu.CompilerParams(vmem_limit_bytes=16 << 20),
        cost_estimate=QUICK,
    )(mine, theirs, *parts)


def on_device(
    features, weight, bias_terms, blocks, block_rows, block_cols, tile_slot_count, cotangent
):
    own_rows, channels = features.shape
    row_devices, col_devices = lax.axis_size("row"), lax.axis_size("col")
    per = own_rows // BS
    row_blocks, column_blocks = per * col_devices, per * row_devices
    inner = inner_of(row_devices)
    on_row = tree(row_devices // inner, inner, True)
    on_col = tree(col_devices // 2, 2, False)
    across = col_devices - 2
    on_col = [route for route in on_col if route[0] != across]

    depths = {d: depth_of(d, on_row) for d, _ in on_row}
    short = [d for d, p in on_row if p and p < inner and d >= inner]
    chain = [max(depths, key=lambda d: (depths[d], d not in short))]
    while chain[-1]:
        chain.append(dict(on_row)[chain[-1]])
    first = [d for d in depths if depths[d] == max(depths.values())]
    late_columns = [d for d, p in on_row if depths[d] == max(depths.values()) or d in short]

    bits = widths(blocks.shape[0], row_blocks, column_blocks)
    indices = jnp.concatenate([block_rows[:, 0], block_cols[:, 0], tile_slot_count[0]])
    table, held = prep(indices, blocks, per, bits, late_columns, first)
    pieces = {0: features.reshape(per, BS, channels)}
    queue = Queue()
    for offset, parent in sorted(
        on_row,
        key=lambda r: (
            depths[r[0]], r[0] not in chain, (r[0] ^ r[1]) < inner
        ),
    ):
        pieces[offset] = queue.swap(pieces[parent], "row", offset ^ parent, f"features_{offset}")
        if offset == chain[-2]:
            pieces[offset] = after(pieces[offset], table)
    other_cotangent = queue.swap(cotangent, "col", across, "cotangent")
    early = {d: p for d, p in pieces.items() if d not in late_columns}
    late = {d: p for d, p in pieces.items() if d in late_columns}
    total = sparse(FORWARD_EARLY, bits, table, held, early, "row", "col", column_blocks, row_blocks)
    sums = sparse(
        FORWARD_LATE, bits, table, held, late, "row", "col", column_blocks, row_blocks, total,
        {d: jnp.float32 if d in (0, across) else jnp.bfloat16 for d in range(col_devices)}, per,
    )

    terms = collect(dict(enumerate(sums)), "col", on_col)
    terms[0][0] = after(terms[0][0], other_cotangent)
    mine = add(terms[0]).astype(jnp.bfloat16)
    others = add(terms[across]).astype(jnp.bfloat16)
    to_mine, to_others = swap(others, "col", across), swap(mine, "col", across)
    scaling = 1.0 / math.sqrt(own_rows * row_devices * col_devices)
    bias = bias_terms.reshape(1, -1)
    hidden, back, other_back, grads = dense(
        weight, bias,
        [(mine, to_mine, cotangent), (others, to_others, other_cotangent)], scaling,
    )
    grads = grads + swap(grads, "col", 1)
    for mask in mirror_masks(col_devices // 2)[1:]:
        grads = grads + swap(grads, "col", 2 * mask)

    rows = spread({0: back, across: other_back}, "col", on_col)
    rows[0] = after(rows[0], grads)
    types = {d: jnp.bfloat16 if d else jnp.float32 for d in range(row_devices)}
    rest = [d for d in range(row_devices) if d not in first]
    leave_first, leave_last = [
        sparse(
            which, bits, table, held, rows, "col", "row", row_blocks, column_blocks,
            None, {d: types[d] for d in chosen}, per,
        )
        for which, chosen in ((BACK_FIRST, first), (BACK_LAST, rest))
    ]
    sums = dict(zip(first, leave_first)) | dict(zip(rest, leave_last))

    terms = {d: [p] for d, p in sums.items()}
    queue = Queue()
    top = chain[-2]
    order = sorted(
        on_row, key=lambda r: (-depths[r[0]], r[0] != top ^ 1, r[0] not in chain, r[0])
    )
    masks = [d ^ parent for d, parent in zip(chain, chain[1:])]
    masks = masks[:1] + masks[-1:] + masks[1:-1]
    masks += [m for m in mirror_masks(inner) if m not in masks]
    masks += [inner * m for m in mirror_masks(row_devices // inner) if inner * m not in masks]
    mine, theirs = grads.astype(jnp.bfloat16), None
    for n, (offset, parent) in enumerate(order):
        total = add(terms.pop(offset)).astype(jnp.bfloat16)
        terms[parent].append(queue.swap(total, "row", offset ^ parent, f"sums_{offset}"))
        if n + 1 < len(order) and depths[order[n + 1][0]] == depths[offset]:
            continue
        for mask in masks[:1] if n + 1 < len(order) else masks:
            if theirs is not None:
                mine = add([mine, after(theirs, queue.last)]).astype(jnp.bfloat16)
            theirs = queue.swap(mine, "row", mask, f"gradients_{mask}")
        masks = masks[1:]
    feat_grad, weight_grad, bias_grad = finish(terms[0], mine, theirs)
    return hidden, feat_grad, weight_grad, bias_grad.reshape(-1)


def solution(mesh):
    return jax.shard_map(
        on_device,
        mesh=mesh,
        in_specs=(
            P(("col", "row"), None),
            P(),
            P(),
            P("row", "col", None),
            P("row", "col"),
            P("row", "col"),
            P("row", "col"),
            P(("row", "col"), None),
        ),
        out_specs=(P(("row", "col"), None), P(("col", "row"), None), P(), P()),
        check_vma=False,
    )
```

```python
from functools import partial
import math

import jax
import jax.numpy as jnp
import numpy as np
from jax import lax
from jax.experimental import pallas as pl
from jax.experimental.pallas import tpu as pltpu
from jax.sharding import PartitionSpec as P

BS = 128
C0 = 0.7978845608
C1 = 0.044715
QUICK = pl.CostEstimate(flops=1, bytes_accessed=1, transcendentals=0)
ANY = pl.BlockSpec(memory_space=pl.ANY)
HBM = pl.BlockSpec(memory_space=pltpu.HBM)
SMEM = pl.BlockSpec(memory_space=pltpu.SMEM)
VMEM = pl.BlockSpec(memory_space=pltpu.VMEM)


def mirror_masks(size):
    masks = []
    while size > 1:
        masks.append(size - 1)
        size //= 2
    return masks


def steps_to(offset, masks):
    steps = []
    for mask in masks:
        if offset & ((mask + 1) >> 1):
            steps.append(mask)
            offset ^= mask
    return steps


def tree(outer, inner, shortcut):
    assert outer & (outer - 1) == 0 and inner & (inner - 1) == 0
    outer_masks, inner_masks = mirror_masks(outer), mirror_masks(inner)
    found = []
    for o in range(outer):
        o_steps = steps_to(o, outer_masks)
        for i in range(inner):
            i_steps = steps_to(i, inner_masks)
            if o == 0 and i == 0:
                continue
            short = bool(i) and shortcut and o == 1
            if i and not short:
                parent = (o, i ^ i_steps[-1])
            else:
                parent = (o ^ o_steps[-1], i)
            depth = len(o_steps) + len(i_steps)
            found.append((depth, short, -o, i, parent))
    found.sort()
    return [(-o * inner + i, parent[0] * inner + parent[1]) for _, _, o, i, parent in found]


def inner_of(size):
    inner = 1
    while 2 * (2 * inner) * (2 * inner) <= size:
        inner *= 2
    return inner


def depth_of(offset, routes):
    parents = dict(routes)
    depth = 0
    while offset:
        offset, depth = parents[offset], depth + 1
    return depth


def swap(x, axis, mask, name="swap"):
    size = lax.axis_size(axis)
    with jax.named_scope(name):
        return lax.ppermute(x, axis, [(i, i ^ mask) for i in range(size)])


def after(x, *others):
    return lax.optimization_barrier((x,) + others)[0]


class Queue:
    def __init__(self):
        self.last = None

    def swap(self, x, axis, mask, name):
        if self.last is not None:
            x = after(x, self.last)
        self.last = x
        return swap(x, axis, mask, name)


def spread(pieces, axis, routes):
    pieces = dict(pieces)
    for offset, parent in routes:
        pieces[offset] = swap(pieces[parent], axis, offset ^ parent, f"rows_{offset}")
    return pieces


def add(terms):
    total = terms[0].astype(jnp.float32)
    for other in terms[1:]:
        total = total + other.astype(jnp.float32)
    return total


def collect(pieces, axis, routes):
    terms = {d: [p] for d, p in pieces.items()}
    for offset, parent in reversed(routes):
        total = add(terms.pop(offset)).astype(jnp.bfloat16)
        terms[parent].append(swap(total, axis, offset ^ parent, f"aggregate_{offset}"))
    return terms


def unroll_of(slots):
    for u in (8, 4, 2):
        if slots % u == 0:
            return u
    return 1


def member(offset, chosen):
    mask = np.uint32(sum(1 << d for d in chosen)).astype(np.int32)
    return lax.bitwise_and(lax.shift_right_logical(jnp.int32(mask), offset), 1)


FORWARD_EARLY, FORWARD_LATE, BACK_FIRST, BACK_LAST = range(4)


def widths(slots, row_blocks, column_blocks):
    bits = [(n - 1).bit_length() for n in (slots, row_blocks, column_blocks)]
    assert sum(bits) < 32
    return bits


def parts_of(slots):
    return 8 if slots % 8 == 0 else 1


def prep_kernel(per, bits, late, first, indices, blocks, table, held, sem):
    slots = blocks.shape[0]
    parts = parts_of(slots)
    copies = []
    for n in range(parts):
        place = pl.ds(n * (slots // parts), slots // parts)
        copies.append(pltpu.make_async_copy(blocks.at[place], held.at[place], sem.at[n]))
        copies[-1].start()
    row_at = lax.axis_index("row")
    live = indices[2 * slots]

    def step(i, lengths):
        early, late_ones, soon, last = lengths
        for u in range(unroll):
            k = i * unroll + u
            row, col = indices[k], indices[slots + k]
            entry = k + lax.shift_left(row, bits[0]) + lax.shift_left(col, bits[0] + bits[1])
            in_use = (k < live).astype(jnp.int32)
            offset = lax.bitwise_xor(row_at, lax.div(col, per))
            is_late, is_first = member(offset, late), member(offset, first)
            table[jnp.where(is_late == 1, slots - 1 - late_ones, early)] = entry
            table[slots + jnp.where(is_first == 1, soon, slots - 1 - last)] = entry
            early, late_ones = early + (1 - is_late) * in_use, late_ones + is_late * in_use
            soon, last = soon + is_first * in_use, last + (1 - is_first) * in_use
        return early, late_ones, soon, last

    unroll = 4 if slots % 4 == 0 else 1
    lengths = lax.fori_loop(0, lax.div(live + unroll - 1, unroll), step, (jnp.int32(0),) * 4)
    for n, length in enumerate(lengths):
        table[2 * slots + n] = length
    for copy in copies:
        copy.wait()


def prep(indices, blocks, per, bits, late, first):
    slots = blocks.shape[0]
    return pl.pallas_call(
        partial(prep_kernel, per, bits, late, first),
        out_shape=[
            jax.ShapeDtypeStruct((2 * slots + 8,), jnp.int32),
            jax.ShapeDtypeStruct(blocks.shape, blocks.dtype),
        ],
        in_specs=[SMEM, HBM],
        out_specs=[SMEM, VMEM],
        scratch_shapes=[pltpu.SemaphoreType.DMA((parts_of(slots),))],
        compiler_params=pltpu.CompilerParams(vmem_limit_bytes=50 << 20),
        cost_estimate=QUICK,
    )(indices, blocks)


def sparse_kernel(which, bits, offsets, here, there, sums, starts, *refs):
    transposed = which >= BACK_FIRST
    in_table, held = refs[:2]
    pieces, refs = refs[2 : 2 + len(offsets)], refs[2 + len(offsets) :]
    before = None
    if starts:
        before, refs = refs[0], refs[1:]
    if sums is None:
        total, table, source, sem = refs
    else:
        outs, (total, table, source, sem) = refs[: len(sums)], refs[len(sums) :]
    here, there = lax.axis_index(here), lax.axis_index(there)
    slots = held.shape[0]
    unroll = unroll_of(slots)
    per = pieces[0].shape[0]
    copies = [pltpu.make_async_copy(in_table, table, sem.at[len(offsets)])]
    copies[0].start()
    for n, offset in enumerate(offsets):
        at = lax.bitwise_xor(here, offset) * per
        copies.append(
            pltpu.make_async_copy(pieces[n], source.at[pl.ds(at, per)], sem.at[n])
        )
        copies[-1].start()
    places = []
    if sums is not None:
        out_per = outs[0].shape[0]
        places = [
            pl.ds(lax.bitwise_xor(there, d) * out_per, out_per) for d in sums
        ]
    if starts:
        for place in places:
            total[place] = before[place]
    elif places:
        for place, out in zip(places, outs):
            total[place] = jnp.zeros(out.shape, jnp.float32)
    else:
        total[...] = jnp.zeros_like(total)
    sink = total.shape[0] - 1
    for copy in copies:
        copy.wait()
    length = table[2 * slots + which]
    idle = lax.bitwise_xor(here, offsets[0]) * per

    def step(i, carry):
        products, targets = [], []
        for u in range(unroll):
            n = i * unroll + u
            in_use = n < length
            at = jnp.minimum(n, slots - 1)
            if which in (FORWARD_LATE, BACK_LAST):
                at = slots - 1 - at
            entry = jnp.where(in_use, table[slots * transposed + at], 0)
            k = lax.bitwise_and(entry, (1 << bits[0]) - 1)
            row = lax.bitwise_and(lax.shift_right_logical(entry, bits[0]), (1 << bits[1]) - 1)
            col = lax.shift_right_logical(entry, bits[0] + bits[1])
            if transposed:
                source_at, target = row, col
                lhs, rhs = source.at[jnp.where(in_use, source_at, idle)], held.at[k]
            else:
                source_at, target = col, row
                lhs, rhs = held.at[k], source.at[jnp.where(in_use, source_at, idle)]
            products.append(jnp.dot(lhs[...], rhs[...], preferred_element_type=jnp.float32))
            targets.append(jnp.where(in_use, target, sink))
        for product, target in zip(products, targets):
            total[target] = total[target] + product
        return carry

    lax.fori_loop(0, lax.div(length + unroll - 1, unroll), step, 0)
    if sums is not None:
        for out, place in zip(outs, places):
            out[...] = total[place].astype(out.dtype)


def sparse(which, bits, table, held, pieces, here, there, sources, targets, before=None, sums=None, out_per=0):
    offsets = sorted(pieces)
    per = pieces[offsets[0]].shape[0]
    block = held.shape[1:]
    whole = jax.ShapeDtypeStruct((targets + 1,) + block, jnp.float32)
    scratch = [
        pltpu.VMEM(whole.shape, whole.dtype),
        pltpu.SMEM(table.shape, table.dtype),
        pltpu.VMEM((sources,) + block, jnp.bfloat16),
        pltpu.SemaphoreType.DMA((len(offsets) + 1,)),
    ]
    if sums is None:
        out_shape = whole
        scratch.pop(0)
    else:
        out_shape = [jax.ShapeDtypeStruct((out_per,) + block, sums[d]) for d in sums]
    operands = [table, held] + [pieces[d] for d in offsets]
    in_specs = [ANY, VMEM] + [ANY] * len(offsets)
    if before is not None:
        operands.append(before)
        in_specs.append(VMEM)
    size = 2 * BS * BS
    need = size * (held.shape[0] + 2 * sources + 5 * (targets + 1)) + (6 << 20)
    return pl.pallas_call(
        partial(
            sparse_kernel,
            which,
            bits,
            tuple(offsets),
            here,
            there,
            None if sums is None else tuple(sums),
            before is not None,
        ),
        out_shape=out_shape,
        in_specs=in_specs,
        out_specs=jax.tree.map(lambda _: VMEM, out_shape),
        scratch_shapes=scratch,
        compiler_params=pltpu.CompilerParams(vmem_limit_bytes=need),
        cost_estimate=QUICK,
    )(*operands)


def dense_kernel(scaling, own, mine, theirs, weight, bias, cotangent, *outs):
    rows, channels = cotangent.shape[0], mine.shape[-1]
    back, grads = outs[-2:]
    aggregate = mine[...].astype(jnp.float32) + theirs[...].astype(jnp.float32)
    aggregate_b = aggregate.astype(jnp.bfloat16).reshape(rows, channels)
    v = jnp.dot(aggregate_b, weight[...], preferred_element_type=jnp.float32) + bias[...]
    square = v * v
    t = jnp.tanh(C0 * (v + C1 * (v * square)))
    half = 0.5 * (1.0 + t)
    if own:
        outs[0][...] = (v * half).astype(jnp.bfloat16)
    slope = half + (0.5 * v) * (1.0 - t * t) * (C0 * (1.0 + (3.0 * C1) * square))
    dpreact = cotangent[...].astype(jnp.float32) * slope
    dpreact_b = dpreact.astype(jnp.bfloat16)
    for n in range(rows // BS):
        back[n] = lax.dot_general(
            weight[...],
            dpreact_b[n * BS : (n + 1) * BS],
            (((1,), (1,)), ((), ())),
            preferred_element_type=jnp.float32,
        ).astype(jnp.bfloat16)
    grads[:channels] = scaling * lax.dot_general(
        aggregate_b, dpreact_b, (((0,), (0,)), ((), ())), preferred_element_type=jnp.float32
    )
    bias_grad = scaling * jnp.sum(dpreact, axis=0, keepdims=True)
    grads[channels:] = jnp.broadcast_to(bias_grad, (grads.shape[0] - channels, grads.shape[1]))


def dense(mine, theirs, weight, bias, cotangent, scaling, own):
    rows, (channels, units) = cotangent.shape[0], weight.shape
    out_shape = [
        jax.ShapeDtypeStruct((rows // BS, channels, BS), jnp.bfloat16),
        jax.ShapeDtypeStruct((channels + 16, units), jnp.float32),
    ]
    if own:
        out_shape.insert(0, pltpu.VMEM(cotangent.shape, jnp.bfloat16))
    return pl.pallas_call(
        partial(dense_kernel, scaling, own),
        out_shape=out_shape,
        in_specs=[VMEM] * 5,
        out_specs=[VMEM] * len(out_shape),
        compiler_params=pltpu.CompilerParams(vmem_limit_bytes=24 << 20),
        cost_estimate=QUICK,
    )(mine, theirs, weight, bias, cotangent)


def finish_kernel(*refs):
    mine, theirs = refs[:2]
    parts, (out, weight_grad, bias_grad) = refs[2:-3], refs[-3:]
    for n in range(parts[0].shape[0]):
        total = parts[0][n].astype(jnp.float32)
        for part in parts[1:]:
            total = total + part[n].astype(jnp.float32)
        out[n * BS : (n + 1) * BS] = total.T
    grads = mine[...].astype(jnp.float32) + theirs[...].astype(jnp.float32)
    channels = weight_grad.shape[0]
    weight_grad[...] = grads[:channels]
    bias_grad[...] = grads[channels : channels + 1]


def finish(parts, mine, theirs):
    per, channels, nodes = parts[0].shape
    units = mine.shape[1]
    out_shape = [
        jax.ShapeDtypeStruct(shape, jnp.float32)
        for shape in ((per * nodes, channels), (channels, units), (1, units))
    ]
    return pl.pallas_call(
        finish_kernel,
        out_shape=out_shape,
        in_specs=[VMEM] * (len(parts) + 2),
        out_specs=[VMEM] * 3,
        compiler_params=pltpu.CompilerParams(vmem_limit_bytes=16 << 20),
        cost_estimate=QUICK,
    )(mine, theirs, *parts)


def on_device(
    features, weight, bias_terms, blocks, block_rows, block_cols, tile_slot_count, cotangent
):
    own_rows, channels = features.shape
    row_devices, col_devices = lax.axis_size("row"), lax.axis_size("col")
    per = own_rows // BS
    row_blocks, column_blocks = per * col_devices, per * row_devices
    inner = inner_of(row_devices)
    on_row = tree(row_devices // inner, inner, True)
    off_row = tree(row_devices // inner, inner, False)
    on_col = tree(col_devices // 2, 2, False)
    across = col_devices - 2
    on_col = [route for route in on_col if route[0] != across]

    depths = {d: depth_of(d, on_row) for d, _ in on_row}
    short = [d for d, p in on_row if p and p < inner and d >= inner]
    chain = [max(depths, key=lambda d: (depths[d], d not in short))]
    while chain[-1]:
        chain.append(dict(on_row)[chain[-1]])
    first = [d for d in depths if depths[d] == max(depths.values())]
    late_columns = [d for d, p in on_row if depths[d] == max(depths.values()) or d in short]

    bits = widths(blocks.shape[0], row_blocks, column_blocks)
    indices = jnp.concatenate([block_rows[:, 0], block_cols[:, 0], tile_slot_count[0]])
    table, held = prep(indices, blocks, per, bits, late_columns, first)
    pieces = {0: features.reshape(per, BS, channels)}
    queue = Queue()
    for offset, parent in sorted(
        on_row,
        key=lambda r: (
            depths[r[0]], r[0] not in chain, (r[0] ^ r[1]) < inner
        ),
    ):
        pieces[offset] = queue.swap(pieces[parent], "row", offset ^ parent, f"features_{offset}")
        if offset == chain[-2]:
            pieces[offset] = after(pieces[offset], table)
    other_cotangent = queue.swap(cotangent, "col", across, "cotangent")
    early = {d: p for d, p in pieces.items() if d not in late_columns}
    late = {d: p for d, p in pieces.items() if d in late_columns}
    total = sparse(FORWARD_EARLY, bits, table, held, early, "row", "col", column_blocks, row_blocks)
    sums = sparse(
        FORWARD_LATE, bits, table, held, late, "row", "col", column_blocks, row_blocks, total,
        {d: jnp.float32 if d in (0, across) else jnp.bfloat16 for d in range(col_devices)}, per,
    )

    terms = collect(dict(enumerate(sums)), "col", on_col)
    terms[0][0] = after(terms[0][0], other_cotangent)
    mine = add(terms[0]).astype(jnp.bfloat16)
    others = add(terms[across]).astype(jnp.bfloat16)
    to_mine, to_others = swap(others, "col", across), swap(mine, "col", across)
    scaling = 1.0 / math.sqrt(own_rows * row_devices * col_devices)
    bias = bias_terms.reshape(1, -1)
    hidden, back, grads = dense(mine, to_mine, weight, bias, cotangent, scaling, True)
    other_back, other_grads = dense(
        others, to_others, weight, bias, other_cotangent, scaling, False
    )
    grads = grads + other_grads
    grads = grads + swap(grads, "col", 1)
    for mask in mirror_masks(col_devices // 2)[1:]:
        grads = grads + swap(grads, "col", 2 * mask)

    rows = spread({0: back, across: other_back}, "col", on_col)
    types = {d: jnp.bfloat16 if d else jnp.float32 for d in range(row_devices)}
    rest = [d for d in range(row_devices) if d not in first]
    leave_first, leave_last = [
        sparse(
            which, bits, table, held, rows, "col", "row", row_blocks, column_blocks,
            None, {d: types[d] for d in chosen}, per,
        )
        for which, chosen in ((BACK_FIRST, first), (BACK_LAST, rest))
    ]
    sums = dict(zip(first, leave_first)) | dict(zip(rest, leave_last))

    terms = {d: [p] for d, p in sums.items()}
    queue = Queue()
    top = chain[-2]
    stages = {d: depth_of(d, off_row) + (d < inner) for d, _ in off_row}
    order = sorted(
        off_row, key=lambda r: (-stages[r[0]], r[0] != top ^ 1, r[0] not in chain, -r[0])
    )
    masks = [d ^ parent for d, parent in zip(chain, chain[1:])]
    masks = masks[1:] + masks[:1]
    masks += [m for m in mirror_masks(inner) if m not in masks]
    masks += [inner * m for m in mirror_masks(row_devices // inner) if inner * m not in masks]
    mine, theirs = grads.astype(jnp.bfloat16), None
    for n, (offset, parent) in enumerate(order):
        total = add(terms.pop(offset)).astype(jnp.bfloat16)
        terms[parent].append(queue.swap(total, "row", offset ^ parent, f"sums_{offset}"))
        if n + 1 < len(order) and stages[order[n + 1][0]] == stages[offset]:
            continue
        for mask in masks[:1] if n + 1 < len(order) else masks:
            if theirs is not None:
                mine = add([mine, after(theirs, queue.last)]).astype(jnp.bfloat16)
            theirs = queue.swap(mine, "row", mask, f"gradients_{mask}")
        masks = masks[1:]
    feat_grad, weight_grad, bias_grad = finish(terms[0], mine, theirs)
    return hidden, feat_grad, weight_grad, bias_grad.reshape(-1)


def solution(mesh):
    return jax.shard_map(
        on_device,
        mesh=mesh,
        in_specs=(
            P(("col", "row"), None),
            P(),
            P(),
            P("row", "col", None),
            P("row", "col"),
            P("row", "col"),
            P("row", "col"),
            P(("row", "col"), None),
        ),
        out_specs=(P(("row", "col"), None), P(("col", "row"), None), P(), P()),
        check_vma=False,
    )
```

```python
from functools import partial
import functools
import math
import operator

import jax
import jax.numpy as jnp
import numpy as np
from jax import lax
from jax.experimental import pallas as pl
from jax.experimental.pallas import tpu as pltpu
from jax.sharding import PartitionSpec as P

BS = 128
C0 = 0.7978845608
C1 = 0.044715
QUICK = pl.CostEstimate(flops=1, bytes_accessed=1, transcendentals=0)
ANY = pl.BlockSpec(memory_space=pl.ANY)
HBM = pl.BlockSpec(memory_space=pltpu.HBM)
SMEM = pl.BlockSpec(memory_space=pltpu.SMEM)
VMEM = pl.BlockSpec(memory_space=pltpu.VMEM)


def mirror_masks(size):
    masks = []
    while size > 1:
        masks.append(size - 1)
        size //= 2
    return masks


def steps_to(offset, masks):
    steps = []
    for mask in masks:
        if offset & ((mask + 1) >> 1):
            steps.append(mask)
            offset ^= mask
    return steps


def tree(outer, inner):
    found = []
    for o in range(outer):
        for i in range(inner):
            o_steps, i_steps = steps_to(o, mirror_masks(outer)), steps_to(i, mirror_masks(inner))
            if i:
                found.append((len(o_steps) + len(i_steps), o * inner + i, o * inner + (i ^ i_steps[-1])))
            elif o:
                found.append((len(o_steps), o * inner, (o ^ o_steps[-1]) * inner))
    return [(offset, parent) for _, offset, parent in sorted(found)]


def inner_of(size):
    inner = 1
    while 2 * (2 * inner) * (2 * inner) <= size:
        inner *= 2
    return inner


def offset_of(code, steps):
    chosen = [masks for n, masks in enumerate(steps) if code >> n & 1]
    return tuple(functools.reduce(operator.xor, masks) for masks in zip(*chosen, strict=True)) or (0, 0)


def last_step(code):
    step = code.bit_length() - 1
    return code ^ 1 << step, step


def swap(x, axis, mask, name="swap"):
    size = lax.axis_size(axis)
    with jax.named_scope(name):
        return lax.ppermute(x, axis, [(i, i ^ mask) for i in range(size)])


def row_swap(x, masks, name="swap"):
    rows, cols = lax.axis_size("row"), lax.axis_size("col")
    pairs = [(i * cols + j, (i ^ masks[j % 2]) * cols + j) for i in range(rows) for j in range(cols)]
    with jax.named_scope(name):
        return lax.ppermute(x, ("row", "col"), pairs)


def after(x, *others):
    return lax.optimization_barrier((x,) + others)[0]


class Queue:
    def __init__(self):
        self.last = None

    def tie(self, x):
        if self.last is not None:
            x = after(x, self.last)
        self.last = x
        return x


def spread(pieces, axis, routes):
    pieces = dict(pieces)
    for offset, parent in routes:
        pieces[offset] = swap(pieces[parent], axis, offset ^ parent, f"rows_{offset}")
    return pieces


def add(terms):
    total = terms[0].astype(jnp.float32)
    for other in terms[1:]:
        total = total + other.astype(jnp.float32)
    return total


def collect(pieces, axis, routes):
    terms = {d: [p] for d, p in pieces.items()}
    for offset, parent in reversed(routes):
        total = add(terms.pop(offset)).astype(jnp.bfloat16)
        terms[parent].append(swap(total, axis, offset ^ parent, f"aggregate_{offset}"))
    return terms


def unroll_of(slots):
    for u in (8, 4, 2):
        if slots % u == 0:
            return u
    return 1


def core_at():
    return lax.rem(lax.axis_index("col"), 2)


def by_core(pair):
    return pair[0] if pair[0] == pair[1] else jnp.where(core_at() == 0, pair[0], pair[1])


def member(offset, chosen):
    masks = [np.uint32(sum(1 << pair[core] for pair in chosen)).astype(np.int32) for core in (0, 1)]
    mask = jnp.where(core_at() == 0, jnp.int32(masks[0]), jnp.int32(masks[1]))
    return lax.bitwise_and(lax.shift_right_logical(mask, offset), 1)


FORWARD_EARLY, FORWARD_LATE, BACK_FIRST, BACK_LAST = range(4)


def widths(slots, row_blocks, column_blocks):
    bits = [(n - 1).bit_length() for n in (slots, row_blocks, column_blocks)]
    assert sum(bits) < 32
    return bits


def parts_of(slots):
    return 2 if slots % 2 == 0 else 1


def prep_kernel(per, bits, late, first, indices, blocks, table, held, sem):
    slots = blocks.shape[0]
    parts = parts_of(slots)
    copies = []
    for n in range(parts):
        place = pl.ds(n * (slots // parts), slots // parts)
        copies.append(pltpu.make_async_copy(blocks.at[place], held.at[place], sem.at[n]))
        copies[-1].start()
    row_at = lax.axis_index("row")
    live = indices[2 * slots]

    def step(i, lengths):
        early, late_ones, soon, last = lengths
        for u in range(unroll):
            k = i * unroll + u
            row, col = indices[k], indices[slots + k]
            entry = k + lax.shift_left(row, bits[0]) + lax.shift_left(col, bits[0] + bits[1])
            in_use = (k < live).astype(jnp.int32)
            offset = lax.bitwise_xor(row_at, lax.div(col, per))
            is_late, is_first = member(offset, late), member(offset, first)
            table[jnp.where(is_late == 1, slots - 1 - late_ones, early)] = entry
            table[slots + jnp.where(is_first == 1, soon, slots - 1 - last)] = entry
            early, late_ones = early + (1 - is_late) * in_use, late_ones + is_late * in_use
            soon, last = soon + is_first * in_use, last + (1 - is_first) * in_use
        return early, late_ones, soon, last

    unroll = 4 if slots % 4 == 0 else 1
    lengths = lax.fori_loop(0, lax.div(live + unroll - 1, unroll), step, (jnp.int32(0),) * 4)
    for n, length in enumerate(lengths):
        table[2 * slots + n] = length
    for copy in copies:
        copy.wait()


def prep(indices, blocks, per, bits, late, first):
    slots = blocks.shape[0]
    return pl.pallas_call(
        partial(prep_kernel, per, bits, late, first),
        out_shape=[
            jax.ShapeDtypeStruct((2 * slots + 8,), jnp.int32),
            jax.ShapeDtypeStruct(blocks.shape, blocks.dtype),
        ],
        in_specs=[SMEM, HBM],
        out_specs=[SMEM, VMEM],
        scratch_shapes=[pltpu.SemaphoreType.DMA((parts_of(slots),))],
        compiler_params=pltpu.CompilerParams(vmem_limit_bytes=50 << 20),
        cost_estimate=QUICK,
    )(indices, blocks)


def sparse_kernel(which, bits, offsets, here, there, sums, starts, *refs):
    transposed = which >= BACK_FIRST
    in_table, held = refs[:2]
    pieces, refs = refs[2 : 2 + len(offsets)], refs[2 + len(offsets) :]
    before = None
    if starts:
        before, refs = refs[0], refs[1:]
    if sums is None:
        total, table, source, sem = refs
    else:
        outs, (total, table, source, sem) = refs[: len(sums)], refs[len(sums) :]
    here, there = lax.axis_index(here), lax.axis_index(there)
    slots = held.shape[0]
    unroll = unroll_of(slots)
    per = pieces[0].shape[0]
    copies = [pltpu.make_async_copy(in_table, table, sem.at[len(offsets)])]
    copies[0].start()
    for n, offset in enumerate(offsets):
        at = lax.bitwise_xor(here, by_core(offset)) * per
        copies.append(
            pltpu.make_async_copy(pieces[n], source.at[pl.ds(at, per)], sem.at[n])
        )
        copies[-1].start()
    places = []
    if sums is not None:
        out_per = outs[0].shape[0]
        places = [
            pl.ds(lax.bitwise_xor(there, by_core(d)) * out_per, out_per) for d in sums
        ]
    if starts:
        for place in places:
            total[place] = before[place]
    elif places:
        for place, out in zip(places, outs):
            total[place] = jnp.zeros(out.shape, jnp.float32)
    else:
        total[...] = jnp.zeros_like(total)
    sink = total.shape[0] - 1
    for copy in copies:
        copy.wait()
    length = table[2 * slots + which]
    idle = lax.bitwise_xor(here, by_core(offsets[0])) * per

    def step(i, carry):
        products, targets = [], []
        for u in range(unroll):
            n = i * unroll + u
            in_use = n < length
            at = jnp.minimum(n, slots - 1)
            if which in (FORWARD_LATE, BACK_LAST):
                at = slots - 1 - at
            entry = jnp.where(in_use, table[slots * transposed + at], 0)
            k = lax.bitwise_and(entry, (1 << bits[0]) - 1)
            row = lax.bitwise_and(lax.shift_right_logical(entry, bits[0]), (1 << bits[1]) - 1)
            col = lax.shift_right_logical(entry, bits[0] + bits[1])
            if transposed:
                source_at, target = row, col
                lhs, rhs = source.at[jnp.where(in_use, source_at, idle)], held.at[k]
            else:
                source_at, target = col, row
                lhs, rhs = held.at[k], source.at[jnp.where(in_use, source_at, idle)]
            products.append(jnp.dot(lhs[...], rhs[...], preferred_element_type=jnp.float32))
            targets.append(jnp.where(in_use, target, sink))
        for product, target in zip(products, targets):
            total[target] = total[target] + product
        return carry

    lax.fori_loop(0, lax.div(length + unroll - 1, unroll), step, 0)
    if sums is not None:
        for out, place in zip(outs, places):
            out[...] = total[place].astype(out.dtype)


def sparse(which, bits, table, held, pieces, here, there, sources, targets, before=None, sums=None, out_per=0):
    offsets = sorted(pieces)
    per = pieces[offsets[0]].shape[0]
    block = held.shape[1:]
    whole = jax.ShapeDtypeStruct((targets + 1,) + block, jnp.float32)
    scratch = [
        pltpu.VMEM(whole.shape, whole.dtype),
        pltpu.SMEM(table.shape, table.dtype),
        pltpu.VMEM((sources,) + block, jnp.bfloat16),
        pltpu.SemaphoreType.DMA((len(offsets) + 1,)),
    ]
    if sums is None:
        out_shape = whole
        scratch.pop(0)
    else:
        out_shape = [jax.ShapeDtypeStruct((out_per,) + block, sums[d]) for d in sums]
    operands = [table, held] + [pieces[d] for d in offsets]
    in_specs = [ANY, VMEM] + [ANY] * len(offsets)
    if before is not None:
        operands.append(before)
        in_specs.append(VMEM)
    size = 2 * BS * BS
    need = size * (held.shape[0] + 2 * sources + 5 * (targets + 1)) + (6 << 20)
    return pl.pallas_call(
        partial(
            sparse_kernel,
            which,
            bits,
            tuple(offsets),
            here,
            there,
            None if sums is None else tuple(sums),
            before is not None,
        ),
        out_shape=out_shape,
        in_specs=in_specs,
        out_specs=jax.tree.map(lambda _: VMEM, out_shape),
        scratch_shapes=scratch,
        compiler_params=pltpu.CompilerParams(vmem_limit_bytes=need),
        cost_estimate=QUICK,
    )(*operands)


def dense_kernel(scaling, own, mine, theirs, weight, bias, cotangent, *outs):
    rows, channels = cotangent.shape[0], mine.shape[-1]
    back, grads = outs[-2:]
    aggregate = mine[...].astype(jnp.float32) + theirs[...].astype(jnp.float32)
    aggregate_b = aggregate.astype(jnp.bfloat16).reshape(rows, channels)
    v = jnp.dot(aggregate_b, weight[...], preferred_element_type=jnp.float32) + bias[...]
    square = v * v
    t = jnp.tanh(C0 * (v + C1 * (v * square)))
    half = 0.5 * (1.0 + t)
    if own:
        outs[0][...] = (v * half).astype(jnp.bfloat16)
    slope = half + (0.5 * v) * (1.0 - t * t) * (C0 * (1.0 + (3.0 * C1) * square))
    dpreact = cotangent[...].astype(jnp.float32) * slope
    dpreact_b = dpreact.astype(jnp.bfloat16)
    for n in range(rows // BS):
        back[n] = lax.dot_general(
            weight[...],
            dpreact_b[n * BS : (n + 1) * BS],
            (((1,), (1,)), ((), ())),
            preferred_element_type=jnp.float32,
        ).astype(jnp.bfloat16)
    grads[:channels] = scaling * lax.dot_general(
        aggregate_b, dpreact_b, (((0,), (0,)), ((), ())), preferred_element_type=jnp.float32
    )
    bias_grad = scaling * jnp.sum(dpreact, axis=0, keepdims=True)
    grads[channels:] = jnp.broadcast_to(bias_grad, (grads.shape[0] - channels, grads.shape[1]))


def dense(mine, theirs, weight, bias, cotangent, scaling, own):
    rows, (channels, units) = cotangent.shape[0], weight.shape
    out_shape = [
        jax.ShapeDtypeStruct((rows // BS, channels, BS), jnp.bfloat16),
        jax.ShapeDtypeStruct((channels + 16, units), jnp.float32),
    ]
    if own:
        out_shape.insert(0, pltpu.VMEM(cotangent.shape, jnp.bfloat16))
    return pl.pallas_call(
        partial(dense_kernel, scaling, own),
        out_shape=out_shape,
        in_specs=[VMEM] * 5,
        out_specs=[VMEM] * len(out_shape),
        compiler_params=pltpu.CompilerParams(vmem_limit_bytes=24 << 20),
        cost_estimate=QUICK,
    )(mine, theirs, weight, bias, cotangent)


def finish_kernel(*refs):
    mine, theirs = refs[:2]
    parts, (out, weight_grad, bias_grad) = refs[2:-3], refs[-3:]
    for n in range(parts[0].shape[0]):
        total = parts[0][n].astype(jnp.float32)
        for part in parts[1:]:
            total = total + part[n].astype(jnp.float32)
        out[n * BS : (n + 1) * BS] = total.T
    grads = mine[...].astype(jnp.float32) + theirs[...].astype(jnp.float32)
    channels = weight_grad.shape[0]
    weight_grad[...] = grads[:channels]
    bias_grad[...] = grads[channels : channels + 1]


def finish(parts, mine, theirs):
    per, channels, nodes = parts[0].shape
    units = mine.shape[1]
    out_shape = [
        jax.ShapeDtypeStruct(shape, jnp.float32)
        for shape in ((per * nodes, channels), (channels, units), (1, units))
    ]
    return pl.pallas_call(
        finish_kernel,
        out_shape=out_shape,
        in_specs=[VMEM] * (len(parts) + 2),
        out_specs=[VMEM] * 3,
        compiler_params=pltpu.CompilerParams(vmem_limit_bytes=16 << 20),
        cost_estimate=QUICK,
    )(mine, theirs, *parts)


def on_device(
    features, weight, bias_terms, blocks, block_rows, block_cols, tile_slot_count, cotangent
):
    own_rows, channels = features.shape
    row_devices, col_devices = lax.axis_size("row"), lax.axis_size("col")
    per = own_rows // BS
    row_blocks, column_blocks = per * col_devices, per * row_devices
    inner = inner_of(row_devices)
    on_col = tree(col_devices // 2, 2)
    across = col_devices - 2
    on_col = [route for route in on_col if route[0] != across]

    outer_steps = [inner * mask for mask in mirror_masks(row_devices // inner)]
    inner_steps = mirror_masks(inner)
    there = list(zip(outer_steps + inner_steps, outer_steps[:-1] + inner_steps + outer_steps[-1:]))
    back_steps = [(mask, mask) for mask in outer_steps + inner_steps]
    count = len(there)
    assert 1 << count == row_devices
    codes = sorted(range(1, row_devices), key=lambda code: (code.bit_count(), code))
    late_codes = codes[-(row_devices // 4) :]
    first_codes = codes[-1:]
    late_columns = [offset_of(code, there) for code in late_codes]
    first = [offset_of(code, back_steps) for code in first_codes]
    bits = widths(blocks.shape[0], row_blocks, column_blocks)
    indices = jnp.concatenate([block_rows, block_cols, tile_slot_count], axis=0)[:, 0]
    table, held = prep(indices, blocks, per, bits, late_columns, first)
    pieces = {0: features.reshape(per, BS, channels)}
    queue = Queue()
    for code in codes:
        parent, step = last_step(code)
        pieces[code] = row_swap(queue.tie(pieces[parent]), there[step], f"features_{code}")
        if code == 1:
            pieces[code] = after(pieces[code], table)
    other_cotangent = swap(queue.tie(cotangent), "col", across, "cotangent")
    early = {offset_of(c, there): p for c, p in pieces.items() if c not in late_codes}
    late = {offset_of(c, there): p for c, p in pieces.items() if c in late_codes}
    total = sparse(FORWARD_EARLY, bits, table, held, early, "row", "col", column_blocks, row_blocks)
    sums = sparse(
        FORWARD_LATE, bits, table, held, late, "row", "col", column_blocks, row_blocks, total,
        {(d, d): jnp.float32 if d in (0, across) else jnp.bfloat16 for d in range(col_devices)}, per,
    )

    terms = collect(dict(enumerate(sums)), "col", on_col)
    terms[0][0] = after(terms[0][0], other_cotangent)
    mine = add(terms[0]).astype(jnp.bfloat16)
    others = add(terms[across]).astype(jnp.bfloat16)
    to_mine, to_others = swap(others, "col", across), swap(mine, "col", across)
    scaling = 1.0 / math.sqrt(own_rows * row_devices * col_devices)
    bias = bias_terms.reshape(1, -1)
    hidden, back, grads = dense(mine, to_mine, weight, bias, cotangent, scaling, True)
    other_back, other_grads = dense(
        others, to_others, weight, bias, other_cotangent, scaling, False
    )
    grads = grads + other_grads
    grads = grads + swap(grads, "col", 1)
    for mask in mirror_masks(col_devices // 2)[1:]:
        grads = grads + swap(grads, "col", 2 * mask)

    rows = spread({0: back, across: other_back}, "col", on_col)
    types = {code: jnp.bfloat16 if code else jnp.float32 for code in range(row_devices)}
    rest = [code for code in range(row_devices) if code not in first_codes]
    rows = {(d, d): p for d, p in rows.items()}
    leave_first, leave_last = [
        sparse(
            which, bits, table, held, rows, "col", "row", row_blocks, column_blocks,
            None, {offset_of(c, back_steps): types[c] for c in chosen}, per,
        )
        for which, chosen in ((BACK_FIRST, first_codes), (BACK_LAST, rest))
    ]
    sums = dict(zip(first_codes, leave_first)) | dict(zip(rest, leave_last))
    whole_way = [(1 << n) - 1 for n in range(1, count + 1)]
    outer_codes = (1 << len(outer_steps)) - 1
    stages = {code: code.bit_count() + (code & outer_codes == 0) for code in codes}
    order = sorted(
        codes, key=lambda code: (-stages[code], code != 1 + (1 << count - 1), code not in whole_way, -code)
    )
    grad_steps = list(range(count - 2, -1, -1)) + [count - 1]
    terms = {code: [p] for code, p in sums.items()}
    queue = Queue()
    mine, theirs = grads.astype(jnp.bfloat16), None
    for n, code in enumerate(order):
        parent, step = last_step(code)
        total = add(terms.pop(code)).astype(jnp.bfloat16)
        terms[parent].append(row_swap(queue.tie(total), back_steps[step], f"sums_{code}"))
        ends = n + 1 == len(order)
        if not ends and stages[order[n + 1]] == stages[code]:
            continue
        for step in grad_steps if ends else grad_steps[:1]:
            if theirs is not None:
                mine = add([mine, after(theirs, queue.last)]).astype(jnp.bfloat16)
            theirs = row_swap(queue.tie(mine), back_steps[step], f"gradients_{step}")
        grad_steps = grad_steps[1:]
    feat_grad, weight_grad, bias_grad = finish(terms[0], mine, theirs)
    return hidden, feat_grad, weight_grad, bias_grad.reshape(-1)


def solution(mesh):
    return jax.shard_map(
        on_device,
        mesh=mesh,
        in_specs=(
            P(("col", "row"), None),
            P(),
            P(),
            P("row", "col", None),
            P("row", "col"),
            P("row", "col"),
            P("row", "col"),
            P(("row", "col"), None),
        ),
        out_specs=(P(("row", "col"), None), P(("col", "row"), None), P(), P()),
        check_vma=False,
    )
```

```python
from functools import partial
import functools
import math
import operator

import jax
import jax.numpy as jnp
import numpy as np
from jax import lax
from jax.experimental import pallas as pl
from jax.experimental.pallas import tpu as pltpu
from jax.sharding import PartitionSpec as P

BS = 128
C0 = 0.7978845608
C1 = 0.044715
QUICK = pl.CostEstimate(flops=1, bytes_accessed=1, transcendentals=0)
ANY = pl.BlockSpec(memory_space=pl.ANY)
HBM = pl.BlockSpec(memory_space=pltpu.HBM)
SMEM = pl.BlockSpec(memory_space=pltpu.SMEM)
VMEM = pl.BlockSpec(memory_space=pltpu.VMEM)


def mirror_masks(size):
    masks = []
    while size > 1:
        masks.append(size - 1)
        size //= 2
    return masks


def steps_to(offset, masks):
    steps = []
    for mask in masks:
        if offset & ((mask + 1) >> 1):
            steps.append(mask)
            offset ^= mask
    return steps


def tree(outer, inner):
    found = []
    for o in range(outer):
        for i in range(inner):
            o_steps, i_steps = steps_to(o, mirror_masks(outer)), steps_to(i, mirror_masks(inner))
            if i:
                found.append((len(o_steps) + len(i_steps), o * inner + i, o * inner + (i ^ i_steps[-1])))
            elif o:
                found.append((len(o_steps), o * inner, (o ^ o_steps[-1]) * inner))
    return [(offset, parent) for _, offset, parent in sorted(found)]


def inner_of(size):
    inner = 1
    while 2 * (2 * inner) * (2 * inner) <= size:
        inner *= 2
    return inner


def offset_of(code, steps):
    chosen = [masks for n, masks in enumerate(steps) if code >> n & 1]
    return tuple(functools.reduce(operator.xor, masks) for masks in zip(*chosen, strict=True)) or (0, 0)


def last_step(code):
    step = code.bit_length() - 1
    return code ^ 1 << step, step


def swap(x, axis, mask, name="swap"):
    size = lax.axis_size(axis)
    with jax.named_scope(name):
        return lax.ppermute(x, axis, [(i, i ^ mask) for i in range(size)])


def row_swap(x, masks, name="swap"):
    rows, cols = lax.axis_size("row"), lax.axis_size("col")
    pairs = [(i * cols + j, (i ^ masks[j % 2]) * cols + j) for i in range(rows) for j in range(cols)]
    with jax.named_scope(name):
        return lax.ppermute(x, ("row", "col"), pairs)


def after(x, *others):
    return lax.optimization_barrier((x,) + others)[0]


class Queue:
    def __init__(self):
        self.last = None

    def tie(self, x):
        if self.last is not None:
            x = after(x, self.last)
        self.last = x
        return x


def spread(pieces, axis, routes):
    pieces = dict(pieces)
    for offset, parent in routes:
        pieces[offset] = swap(pieces[parent], axis, offset ^ parent, f"rows_{offset}")
    return pieces


def add(terms):
    total = terms[0].astype(jnp.float32)
    for other in terms[1:]:
        total = total + other.astype(jnp.float32)
    return total


def collect(pieces, axis, routes):
    terms = {d: [p] for d, p in pieces.items()}
    for offset, parent in reversed(routes):
        total = add(terms.pop(offset)).astype(jnp.bfloat16)
        terms[parent].append(swap(total, axis, offset ^ parent, f"aggregate_{offset}"))
    return terms


def unroll_of(slots):
    for u in (8, 4, 2):
        if slots % u == 0:
            return u
    return 1


def core_at():
    return lax.rem(lax.axis_index("col"), 2)


def by_core(pair):
    return pair[0] if pair[0] == pair[1] else jnp.where(core_at() == 0, pair[0], pair[1])


def member(offset, chosen):
    masks = [np.uint32(sum(1 << pair[core] for pair in chosen)).astype(np.int32) for core in (0, 1)]
    mask = jnp.where(core_at() == 0, jnp.int32(masks[0]), jnp.int32(masks[1]))
    return lax.bitwise_and(lax.shift_right_logical(mask, offset), 1)


FORWARD_EARLY, FORWARD_LATE, BACK_FIRST, BACK_LAST = range(4)


def widths(slots, row_blocks, column_blocks):
    bits = [(n - 1).bit_length() for n in (slots, row_blocks, column_blocks)]
    assert sum(bits) < 32
    return bits


def parts_of(slots):
    return 2 if slots % 2 == 0 else 1


def prep_kernel(
    per, bits, late, first, in_rows, in_cols, live_slots, blocks, table, held, rows, cols, sem, small_sem
):
    slots = blocks.shape[0]
    small = [
        pltpu.make_async_copy(source, target, small_sem.at[n])
        for n, (source, target) in enumerate(((in_rows, rows), (in_cols, cols)))
    ]
    for copy in small:
        copy.start()
    parts = parts_of(slots)
    copies = []
    for n in range(parts):
        place = pl.ds(n * (slots // parts), slots // parts)
        copies.append(pltpu.make_async_copy(blocks.at[place], held.at[place], sem.at[n]))
        copies[-1].start()
    for copy in small:
        copy.wait()
    row_at = lax.axis_index("row")
    live = live_slots[0, 0]

    def step(i, lengths):
        early, late_ones, soon, last = lengths
        for u in range(unroll):
            k = i * unroll + u
            row, col = rows[k], cols[k]
            entry = k + lax.shift_left(row, bits[0]) + lax.shift_left(col, bits[0] + bits[1])
            in_use = (k < live).astype(jnp.int32)
            offset = lax.bitwise_xor(row_at, lax.div(col, per))
            is_late, is_first = member(offset, late), member(offset, first)
            table[jnp.where(is_late == 1, slots - 1 - late_ones, early)] = entry
            table[slots + jnp.where(is_first == 1, soon, slots - 1 - last)] = entry
            early, late_ones = early + (1 - is_late) * in_use, late_ones + is_late * in_use
            soon, last = soon + is_first * in_use, last + (1 - is_first) * in_use
        return early, late_ones, soon, last

    unroll = 4 if slots % 4 == 0 else 1
    lengths = lax.fori_loop(0, lax.div(live + unroll - 1, unroll), step, (jnp.int32(0),) * 4)
    for n, length in enumerate(lengths):
        table[2 * slots + n] = length
    for copy in copies:
        copy.wait()


def prep(block_rows, block_cols, tile_slot_count, blocks, per, bits, late, first):
    slots = blocks.shape[0]
    in_hbm = partial(pltpu.with_memory_space_constraint, memory_space=pltpu.HBM)
    return pl.pallas_call(
        partial(prep_kernel, per, bits, late, first),
        out_shape=[
            jax.ShapeDtypeStruct((2 * slots + 8,), jnp.int32),
            jax.ShapeDtypeStruct(blocks.shape, blocks.dtype),
        ],
        in_specs=[HBM, HBM, SMEM, HBM],
        out_specs=[SMEM, VMEM],
        scratch_shapes=[
            pltpu.SMEM((slots,), jnp.int32),
            pltpu.SMEM((slots,), jnp.int32),
            pltpu.SemaphoreType.DMA((parts_of(slots),)),
            pltpu.SemaphoreType.DMA((2,)),
        ],
        compiler_params=pltpu.CompilerParams(vmem_limit_bytes=50 << 20),
        cost_estimate=QUICK,
    )(
        in_hbm(block_rows.reshape(slots)), in_hbm(block_cols.reshape(slots)), tile_slot_count, in_hbm(blocks)
    )


def sparse_kernel(which, bits, offsets, here, there, sums, starts, *refs):
    transposed = which >= BACK_FIRST
    in_table, held = refs[:2]
    pieces, refs = refs[2 : 2 + len(offsets)], refs[2 + len(offsets) :]
    before = None
    if starts:
        before, refs = refs[0], refs[1:]
    if sums is None:
        total, table, source, sem = refs
    else:
        outs, (total, table, source, sem) = refs[: len(sums)], refs[len(sums) :]
    here, there = lax.axis_index(here), lax.axis_index(there)
    slots = held.shape[0]
    unroll = unroll_of(slots)
    per = pieces[0].shape[0]
    copies = [pltpu.make_async_copy(in_table, table, sem.at[len(offsets)])]
    copies[0].start()
    for n, offset in enumerate(offsets):
        at = lax.bitwise_xor(here, by_core(offset)) * per
        copies.append(
            pltpu.make_async_copy(pieces[n], source.at[pl.ds(at, per)], sem.at[n])
        )
        copies[-1].start()
    places = []
    if sums is not None:
        out_per = outs[0].shape[0]
        places = [
            pl.ds(lax.bitwise_xor(there, by_core(d)) * out_per, out_per) for d in sums
        ]
    if starts:
        for place in places:
            total[place] = before[place]
    elif places:
        for place, out in zip(places, outs):
            total[place] = jnp.zeros(out.shape, jnp.float32)
    else:
        total[...] = jnp.zeros_like(total)
    sink = total.shape[0] - 1
    for copy in copies:
        copy.wait()
    length = table[2 * slots + which]
    idle = lax.bitwise_xor(here, by_core(offsets[0])) * per

    def step(i, carry):
        products, targets = [], []
        for u in range(unroll):
            n = i * unroll + u
            in_use = n < length
            at = jnp.minimum(n, slots - 1)
            if which in (FORWARD_LATE, BACK_LAST):
                at = slots - 1 - at
            entry = jnp.where(in_use, table[slots * transposed + at], 0)
            k = lax.bitwise_and(entry, (1 << bits[0]) - 1)
            row = lax.bitwise_and(lax.shift_right_logical(entry, bits[0]), (1 << bits[1]) - 1)
            col = lax.shift_right_logical(entry, bits[0] + bits[1])
            if transposed:
                source_at, target = row, col
                lhs, rhs = source.at[jnp.where(in_use, source_at, idle)], held.at[k]
            else:
                source_at, target = col, row
                lhs, rhs = held.at[k], source.at[jnp.where(in_use, source_at, idle)]
            products.append(jnp.dot(lhs[...], rhs[...], preferred_element_type=jnp.float32))
            targets.append(jnp.where(in_use, target, sink))
        for product, target in zip(products, targets):
            total[target] = total[target] + product
        return carry

    lax.fori_loop(0, lax.div(length + unroll - 1, unroll), step, 0)
    if sums is not None:
        for out, place in zip(outs, places):
            out[...] = total[place].astype(out.dtype)


def sparse(which, bits, table, held, pieces, here, there, sources, targets, before=None, sums=None, out_per=0):
    offsets = sorted(pieces)
    per = pieces[offsets[0]].shape[0]
    block = held.shape[1:]
    whole = jax.ShapeDtypeStruct((targets + 1,) + block, jnp.float32)
    scratch = [
        pltpu.VMEM(whole.shape, whole.dtype),
        pltpu.SMEM(table.shape, table.dtype),
        pltpu.VMEM((sources,) + block, jnp.bfloat16),
        pltpu.SemaphoreType.DMA((len(offsets) + 1,)),
    ]
    if sums is None:
        out_shape = whole
        scratch.pop(0)
    else:
        out_shape = [jax.ShapeDtypeStruct((out_per,) + block, sums[d]) for d in sums]
    operands = [table, held] + [pieces[d] for d in offsets]
    in_specs = [ANY, VMEM] + [ANY] * len(offsets)
    if before is not None:
        operands.append(before)
        in_specs.append(VMEM)
    size = 2 * BS * BS
    need = size * (held.shape[0] + 2 * sources + 5 * (targets + 1)) + (6 << 20)
    return pl.pallas_call(
        partial(
            sparse_kernel,
            which,
            bits,
            tuple(offsets),
            here,
            there,
            None if sums is None else tuple(sums),
            before is not None,
        ),
        out_shape=out_shape,
        in_specs=in_specs,
        out_specs=jax.tree.map(lambda _: VMEM, out_shape),
        scratch_shapes=scratch,
        compiler_params=pltpu.CompilerParams(vmem_limit_bytes=need),
        cost_estimate=QUICK,
    )(*operands)


def dense_kernel(scaling, own, mine, theirs, weight, bias, cotangent, *outs):
    rows, channels = cotangent.shape[0], mine.shape[-1]
    back, grads = outs[-2:]
    aggregate = mine[...].astype(jnp.float32) + theirs[...].astype(jnp.float32)
    aggregate_b = aggregate.astype(jnp.bfloat16).reshape(rows, channels)
    v = jnp.dot(aggregate_b, weight[...], preferred_element_type=jnp.float32) + bias[...]
    square = v * v
    t = jnp.tanh(C0 * (v + C1 * (v * square)))
    half = 0.5 * (1.0 + t)
    if own:
        outs[0][...] = (v * half).astype(jnp.bfloat16)
    slope = half + (0.5 * v) * (1.0 - t * t) * (C0 * (1.0 + (3.0 * C1) * square))
    dpreact = cotangent[...].astype(jnp.float32) * slope
    dpreact_b = dpreact.astype(jnp.bfloat16)
    for n in range(rows // BS):
        back[n] = lax.dot_general(
            weight[...],
            dpreact_b[n * BS : (n + 1) * BS],
            (((1,), (1,)), ((), ())),
            preferred_element_type=jnp.float32,
        ).astype(jnp.bfloat16)
    grads[:channels] = scaling * lax.dot_general(
        aggregate_b, dpreact_b, (((0,), (0,)), ((), ())), preferred_element_type=jnp.float32
    )
    bias_grad = scaling * jnp.sum(dpreact, axis=0, keepdims=True)
    grads[channels:] = jnp.broadcast_to(bias_grad, (grads.shape[0] - channels, grads.shape[1]))


def dense(mine, theirs, weight, bias, cotangent, scaling, own):
    rows, (channels, units) = cotangent.shape[0], weight.shape
    out_shape = [
        jax.ShapeDtypeStruct((rows // BS, channels, BS), jnp.bfloat16),
        jax.ShapeDtypeStruct((channels + 16, units), jnp.float32),
    ]
    if own:
        out_shape.insert(0, pltpu.VMEM(cotangent.shape, jnp.bfloat16))
    return pl.pallas_call(
        partial(dense_kernel, scaling, own),
        out_shape=out_shape,
        in_specs=[VMEM] * 5,
        out_specs=[VMEM] * len(out_shape),
        compiler_params=pltpu.CompilerParams(vmem_limit_bytes=24 << 20),
        cost_estimate=QUICK,
    )(mine, theirs, weight, bias, cotangent)


def finish_kernel(*refs):
    mine, theirs = refs[:2]
    parts, (out, weight_grad, bias_grad) = refs[2:-3], refs[-3:]
    for n in range(parts[0].shape[0]):
        total = parts[0][n].astype(jnp.float32)
        for part in parts[1:]:
            total = total + part[n].astype(jnp.float32)
        out[n * BS : (n + 1) * BS] = total.T
    grads = mine[...].astype(jnp.float32) + theirs[...].astype(jnp.float32)
    channels = weight_grad.shape[0]
    weight_grad[...] = grads[:channels]
    bias_grad[...] = grads[channels : channels + 1]


def finish(parts, mine, theirs):
    per, channels, nodes = parts[0].shape
    units = mine.shape[1]
    out_shape = [
        jax.ShapeDtypeStruct(shape, jnp.float32)
        for shape in ((per * nodes, channels), (channels, units), (1, units))
    ]
    return pl.pallas_call(
        finish_kernel,
        out_shape=out_shape,
        in_specs=[VMEM] * (len(parts) + 2),
        out_specs=[VMEM] * 3,
        compiler_params=pltpu.CompilerParams(vmem_limit_bytes=16 << 20),
        cost_estimate=QUICK,
    )(mine, theirs, *parts)


def on_device(
    features, weight, bias_terms, blocks, block_rows, block_cols, tile_slot_count, cotangent
):
    own_rows, channels = features.shape
    row_devices, col_devices = lax.axis_size("row"), lax.axis_size("col")
    per = own_rows // BS
    row_blocks, column_blocks = per * col_devices, per * row_devices
    inner = inner_of(row_devices)
    on_col = tree(col_devices // 2, 2)
    across = col_devices - 2
    on_col = [route for route in on_col if route[0] != across]

    outer_steps = [inner * mask for mask in mirror_masks(row_devices // inner)]
    inner_steps = mirror_masks(inner)
    there = list(zip(outer_steps + inner_steps, outer_steps[:-1] + inner_steps + outer_steps[-1:]))
    back_steps = [(mask, mask) for mask in outer_steps + inner_steps]
    count = len(there)
    assert 1 << count == row_devices
    codes = sorted(range(1, row_devices), key=lambda code: (code.bit_count(), code))
    late_codes = codes[-(row_devices // 4) :]
    first_codes = codes[-1:]
    late_columns = [offset_of(code, there) for code in late_codes]
    first = [offset_of(code, back_steps) for code in first_codes]
    bits = widths(blocks.shape[0], row_blocks, column_blocks)
    table, held = prep(
        block_rows, block_cols, tile_slot_count, blocks, per, bits, late_columns, first
    )
    pieces = {0: features.reshape(per, BS, channels)}
    queue = Queue()
    for code in codes:
        parent, step = last_step(code)
        pieces[code] = row_swap(queue.tie(pieces[parent]), there[step], f"features_{code}")
        if code == 1:
            pieces[code] = after(pieces[code], table)
    other_cotangent = swap(queue.tie(cotangent), "col", across, "cotangent")
    early = {offset_of(c, there): p for c, p in pieces.items() if c not in late_codes}
    late = {offset_of(c, there): p for c, p in pieces.items() if c in late_codes}
    total = sparse(FORWARD_EARLY, bits, table, held, early, "row", "col", column_blocks, row_blocks)
    sums = sparse(
        FORWARD_LATE, bits, table, held, late, "row", "col", column_blocks, row_blocks, total,
        {(d, d): jnp.float32 if d in (0, across) else jnp.bfloat16 for d in range(col_devices)}, per,
    )

    terms = collect(dict(enumerate(sums)), "col", on_col)
    terms[0][0] = after(terms[0][0], other_cotangent)
    mine = add(terms[0]).astype(jnp.bfloat16)
    others = add(terms[across]).astype(jnp.bfloat16)
    to_mine, to_others = swap(others, "col", across), swap(mine, "col", across)
    scaling = 1.0 / math.sqrt(own_rows * row_devices * col_devices)
    bias = bias_terms.reshape(1, -1)
    hidden, back, grads = dense(mine, to_mine, weight, bias, cotangent, scaling, True)
    other_back, other_grads = dense(
        others, to_others, weight, bias, other_cotangent, scaling, False
    )
    grads = grads + other_grads
    grads = grads + swap(grads, "col", 1)
    for mask in mirror_masks(col_devices // 2)[1:]:
        grads = grads + swap(grads, "col", 2 * mask)

    rows = spread({0: back, across: other_back}, "col", on_col)
    types = {code: jnp.bfloat16 if code else jnp.float32 for code in range(row_devices)}
    rest = [code for code in range(row_devices) if code not in first_codes]
    rows = {(d, d): p for d, p in rows.items()}
    leave_first, leave_last = [
        sparse(
            which, bits, table, held, rows, "col", "row", row_blocks, column_blocks,
            None, {offset_of(c, back_steps): types[c] for c in chosen}, per,
        )
        for which, chosen in ((BACK_FIRST, first_codes), (BACK_LAST, rest))
    ]
    sums = dict(zip(first_codes, leave_first)) | dict(zip(rest, leave_last))
    whole_way = [(1 << n) - 1 for n in range(1, count + 1)]
    outer_codes = (1 << len(outer_steps)) - 1
    stages = {code: code.bit_count() + (code & outer_codes == 0) for code in codes}
    order = sorted(
        codes, key=lambda code: (-stages[code], code != 1 + (1 << count - 1), code not in whole_way, -code)
    )
    grad_steps = list(range(count - 2, -1, -1)) + [count - 1]
    terms = {code: [p] for code, p in sums.items()}
    queue = Queue()
    mine, theirs = grads.astype(jnp.bfloat16), None
    for n, code in enumerate(order):
        parent, step = last_step(code)
        total = add(terms.pop(code)).astype(jnp.bfloat16)
        terms[parent].append(row_swap(queue.tie(total), back_steps[step], f"sums_{code}"))
        ends = n + 1 == len(order)
        if not ends and stages[order[n + 1]] == stages[code]:
            continue
        for step in grad_steps if ends else grad_steps[:1]:
            if theirs is not None:
                mine = add([mine, after(theirs, queue.last)]).astype(jnp.bfloat16)
            theirs = row_swap(queue.tie(mine), back_steps[step], f"gradients_{step}")
        grad_steps = grad_steps[1:]
    feat_grad, weight_grad, bias_grad = finish(terms[0], mine, theirs)
    return hidden, feat_grad, weight_grad, bias_grad.reshape(-1)


def solution(mesh):
    return jax.shard_map(
        on_device,
        mesh=mesh,
        in_specs=(
            P(("col", "row"), None),
            P(),
            P(),
            P("row", "col", None),
            P("row", "col"),
            P("row", "col"),
            P("row", "col"),
            P(("row", "col"), None),
        ),
        out_specs=(P(("row", "col"), None), P(("col", "row"), None), P(), P()),
        check_vma=False,
    )
```

```python
from functools import partial
import functools
import math
import operator

import jax
import jax.numpy as jnp
import numpy as np
from jax import lax
from jax.experimental import pallas as pl
from jax.experimental.pallas import tpu as pltpu
from jax.sharding import PartitionSpec as P

BS = 128
C0 = 0.7978845608
C1 = 0.044715
QUICK = pl.CostEstimate(flops=1, bytes_accessed=1, transcendentals=0)
ANY = pl.BlockSpec(memory_space=pl.ANY)
HBM = pl.BlockSpec(memory_space=pltpu.HBM)
SMEM = pl.BlockSpec(memory_space=pltpu.SMEM)
VMEM = pl.BlockSpec(memory_space=pltpu.VMEM)


def mirror_masks(size):
    masks = []
    while size > 1:
        masks.append(size - 1)
        size //= 2
    return masks


def steps_to(offset, masks):
    steps = []
    for mask in masks:
        if offset & ((mask + 1) >> 1):
            steps.append(mask)
            offset ^= mask
    return steps


def tree(outer, inner):
    found = []
    for o in range(outer):
        for i in range(inner):
            o_steps, i_steps = steps_to(o, mirror_masks(outer)), steps_to(i, mirror_masks(inner))
            if i:
                found.append((len(o_steps) + len(i_steps), o * inner + i, o * inner + (i ^ i_steps[-1])))
            elif o:
                found.append((len(o_steps), o * inner, (o ^ o_steps[-1]) * inner))
    return [(offset, parent) for _, offset, parent in sorted(found)]


def inner_of(size):
    inner = 1
    while 2 * (2 * inner) * (2 * inner) <= size:
        inner *= 2
    return inner


def offset_of(code, steps):
    chosen = [masks for n, masks in enumerate(steps) if code >> n & 1]
    return tuple(functools.reduce(operator.xor, masks) for masks in zip(*chosen, strict=True)) or (0, 0)


def last_step(code):
    step = code.bit_length() - 1
    return code ^ 1 << step, step


def swap(x, axis, mask, name="swap"):
    size = lax.axis_size(axis)
    with jax.named_scope(name):
        return lax.ppermute(x, axis, [(i, i ^ mask) for i in range(size)])


def row_swap(x, masks, name="swap"):
    rows, cols = lax.axis_size("row"), lax.axis_size("col")
    pairs = [(i * cols + j, (i ^ masks[j % 2]) * cols + j) for i in range(rows) for j in range(cols)]
    with jax.named_scope(name):
        return lax.ppermute(x, ("row", "col"), pairs)


def after(x, *others):
    return lax.optimization_barrier((x,) + others)[0]


class Queue:
    def __init__(self):
        self.last = None

    def tie(self, x):
        if self.last is not None:
            x = after(x, self.last)
        self.last = x
        return x


def spread(pieces, axis, routes):
    pieces = dict(pieces)
    for offset, parent in routes:
        pieces[offset] = swap(pieces[parent], axis, offset ^ parent, f"rows_{offset}")
    return pieces


def add(terms):
    total = terms[0].astype(jnp.float32)
    for other in terms[1:]:
        total = total + other.astype(jnp.float32)
    return total


def collect(pieces, axis, routes):
    terms = {d: [p] for d, p in pieces.items()}
    for offset, parent in reversed(routes):
        total = add(terms.pop(offset)).astype(jnp.bfloat16)
        terms[parent].append(swap(total, axis, offset ^ parent, f"aggregate_{offset}"))
    return terms


def unroll_of(slots):
    for u in (8, 4, 2):
        if slots % u == 0:
            return u
    return 1


def core_at():
    return lax.rem(lax.axis_index("col"), 2)


def by_core(pair):
    return pair[0] if pair[0] == pair[1] else jnp.where(core_at() == 0, pair[0], pair[1])


def member(offset, chosen):
    masks = [np.uint32(sum(1 << pair[core] for pair in chosen)).astype(np.int32) for core in (0, 1)]
    mask = jnp.where(core_at() == 0, jnp.int32(masks[0]), jnp.int32(masks[1]))
    return lax.bitwise_and(lax.shift_right_logical(mask, offset), 1)


FORWARD_EARLY, FORWARD_LATE, BACK_FIRST, BACK_LAST = range(4)


def widths(slots, row_blocks, column_blocks):
    bits = [(n - 1).bit_length() for n in (slots, row_blocks, column_blocks)]
    assert sum(bits) < 32
    return bits


def parts_of(slots):
    return 2 if slots % 2 == 0 else 1


def prep_kernel(per, bits, late, first, indices, blocks, table, held, sem):
    slots = blocks.shape[0]
    parts = parts_of(slots)
    copies = []
    for n in range(parts):
        place = pl.ds(n * (slots // parts), slots // parts)
        copies.append(pltpu.make_async_copy(blocks.at[place], held.at[place], sem.at[n]))
        copies[-1].start()
    row_at = lax.axis_index("row")
    live = indices[2 * slots]

    def step(i, lengths):
        early, late_ones, soon, last = lengths
        for u in range(unroll):
            k = i * unroll + u
            row, col = indices[k], indices[slots + k]
            entry = k + lax.shift_left(row, bits[0]) + lax.shift_left(col, bits[0] + bits[1])
            in_use = (k < live).astype(jnp.int32)
            offset = lax.bitwise_xor(row_at, lax.div(col, per))
            is_late, is_first = member(offset, late), member(offset, first)
            table[jnp.where(is_late == 1, slots - 1 - late_ones, early)] = entry
            table[slots + jnp.where(is_first == 1, soon, slots - 1 - last)] = entry
            early, late_ones = early + (1 - is_late) * in_use, late_ones + is_late * in_use
            soon, last = soon + is_first * in_use, last + (1 - is_first) * in_use
        return early, late_ones, soon, last

    unroll = 4 if slots % 4 == 0 else 1
    lengths = lax.fori_loop(0, lax.div(live + unroll - 1, unroll), step, (jnp.int32(0),) * 4)
    for n, length in enumerate(lengths):
        table[2 * slots + n] = length
    for copy in copies:
        copy.wait()


def prep(indices, blocks, per, bits, late, first):
    slots = blocks.shape[0]
    return pl.pallas_call(
        partial(prep_kernel, per, bits, late, first),
        out_shape=[
            jax.ShapeDtypeStruct((2 * slots + 8,), jnp.int32),
            jax.ShapeDtypeStruct(blocks.shape, blocks.dtype),
        ],
        in_specs=[SMEM, HBM],
        out_specs=[SMEM, VMEM],
        scratch_shapes=[pltpu.SemaphoreType.DMA((parts_of(slots),))],
        compiler_params=pltpu.CompilerParams(vmem_limit_bytes=50 << 20),
        cost_estimate=QUICK,
    )(indices, blocks)


def sparse_kernel(which, bits, offsets, here, there, sums, starts, *refs):
    transposed = which >= BACK_FIRST
    in_table, held = refs[:2]
    pieces, refs = refs[2 : 2 + len(offsets)], refs[2 + len(offsets) :]
    before = None
    if starts:
        before, refs = refs[0], refs[1:]
    if sums is None:
        total, table, source, sem = refs
    else:
        outs, (total, table, source, sem) = refs[: len(sums)], refs[len(sums) :]
    here, there = lax.axis_index(here), lax.axis_index(there)
    slots = held.shape[0]
    unroll = unroll_of(slots)
    per = pieces[0].shape[0]
    copies = [pltpu.make_async_copy(in_table, table, sem.at[len(offsets)])]
    copies[0].start()
    for n, offset in enumerate(offsets):
        at = lax.bitwise_xor(here, by_core(offset)) * per
        copies.append(
            pltpu.make_async_copy(pieces[n], source.at[pl.ds(at, per)], sem.at[n])
        )
        copies[-1].start()
    places = []
    if sums is not None:
        out_per = outs[0].shape[0]
        places = [
            pl.ds(lax.bitwise_xor(there, by_core(d)) * out_per, out_per) for d in sums
        ]
    if starts:
        for place in places:
            total[place] = before[place]
    elif places:
        for place, out in zip(places, outs):
            total[place] = jnp.zeros(out.shape, jnp.float32)
    else:
        total[...] = jnp.zeros_like(total)
    sink = total.shape[0] - 1
    for copy in copies:
        copy.wait()
    length = table[2 * slots + which]
    idle = lax.bitwise_xor(here, by_core(offsets[0])) * per

    def step(i, carry):
        products, targets = [], []
        for u in range(unroll):
            n = i * unroll + u
            in_use = n < length
            at = jnp.minimum(n, slots - 1)
            if which in (FORWARD_LATE, BACK_LAST):
                at = slots - 1 - at
            entry = jnp.where(in_use, table[slots * transposed + at], 0)
            k = lax.bitwise_and(entry, (1 << bits[0]) - 1)
            row = lax.bitwise_and(lax.shift_right_logical(entry, bits[0]), (1 << bits[1]) - 1)
            col = lax.shift_right_logical(entry, bits[0] + bits[1])
            if transposed:
                source_at, target = row, col
                lhs, rhs = source.at[jnp.where(in_use, source_at, idle)], held.at[k]
            else:
                source_at, target = col, row
                lhs, rhs = held.at[k], source.at[jnp.where(in_use, source_at, idle)]
            products.append(jnp.dot(lhs[...], rhs[...], preferred_element_type=jnp.float32))
            targets.append(jnp.where(in_use, target, sink))
        for product, target in zip(products, targets):
            total[target] = total[target] + product
        return carry

    lax.fori_loop(0, lax.div(length + unroll - 1, unroll), step, 0)
    if sums is not None:
        for out, place in zip(outs, places):
            out[...] = total[place].astype(out.dtype)


def sparse(which, bits, table, held, pieces, here, there, sources, targets, before=None, sums=None, out_per=0):
    offsets = sorted(pieces)
    per = pieces[offsets[0]].shape[0]
    block = held.shape[1:]
    whole = jax.ShapeDtypeStruct((targets + 1,) + block, jnp.float32)
    scratch = [
        pltpu.VMEM(whole.shape, whole.dtype),
        pltpu.SMEM(table.shape, table.dtype),
        pltpu.VMEM((sources,) + block, jnp.bfloat16),
        pltpu.SemaphoreType.DMA((len(offsets) + 1,)),
    ]
    if sums is None:
        out_shape = whole
        scratch.pop(0)
    else:
        out_shape = [jax.ShapeDtypeStruct((out_per,) + block, sums[d]) for d in sums]
    operands = [table, held] + [pieces[d] for d in offsets]
    in_specs = [ANY, VMEM] + [ANY] * len(offsets)
    if before is not None:
        operands.append(before)
        in_specs.append(VMEM)
    size = 2 * BS * BS
    need = size * (held.shape[0] + 2 * sources + 5 * (targets + 1)) + (6 << 20)
    return pl.pallas_call(
        partial(
            sparse_kernel,
            which,
            bits,
            tuple(offsets),
            here,
            there,
            None if sums is None else tuple(sums),
            before is not None,
        ),
        out_shape=out_shape,
        in_specs=in_specs,
        out_specs=jax.tree.map(lambda _: VMEM, out_shape),
        scratch_shapes=scratch,
        compiler_params=pltpu.CompilerParams(vmem_limit_bytes=need),
        cost_estimate=QUICK,
    )(*operands)


def dense_kernel(scaling, own, mine, theirs, weight, bias, cotangent, *outs):
    rows, channels = cotangent.shape[0], mine.shape[-1]
    back, grads = outs[-2:]
    aggregate = mine[...].astype(jnp.float32) + theirs[...].astype(jnp.float32)
    aggregate_b = aggregate.astype(jnp.bfloat16).reshape(rows, channels)
    v = jnp.dot(aggregate_b, weight[...], preferred_element_type=jnp.float32) + bias[...]
    square = v * v
    t = jnp.tanh(C0 * (v + C1 * (v * square)))
    half = 0.5 * (1.0 + t)
    if own:
        outs[0][...] = (v * half).astype(jnp.bfloat16)
    slope = half + (0.5 * v) * (1.0 - t * t) * (C0 * (1.0 + (3.0 * C1) * square))
    dpreact = cotangent[...].astype(jnp.float32) * slope
    dpreact_b = dpreact.astype(jnp.bfloat16)
    for n in range(rows // BS):
        back[n] = lax.dot_general(
            weight[...],
            dpreact_b[n * BS : (n + 1) * BS],
            (((1,), (1,)), ((), ())),
            preferred_element_type=jnp.float32,
        ).astype(jnp.bfloat16)
    grads[:channels] = scaling * lax.dot_general(
        aggregate_b, dpreact_b, (((0,), (0,)), ((), ())), preferred_element_type=jnp.float32
    )
    bias_grad = scaling * jnp.sum(dpreact, axis=0, keepdims=True)
    grads[channels:] = jnp.broadcast_to(bias_grad, (grads.shape[0] - channels, grads.shape[1]))


def dense(mine, theirs, weight, bias, cotangent, scaling, own):
    rows, (channels, units) = cotangent.shape[0], weight.shape
    out_shape = [
        jax.ShapeDtypeStruct((rows // BS, channels, BS), jnp.bfloat16),
        jax.ShapeDtypeStruct((channels + 16, units), jnp.float32),
    ]
    if own:
        out_shape.insert(0, pltpu.VMEM(cotangent.shape, jnp.bfloat16))
    return pl.pallas_call(
        partial(dense_kernel, scaling, own),
        out_shape=out_shape,
        in_specs=[VMEM] * 5,
        out_specs=[VMEM] * len(out_shape),
        compiler_params=pltpu.CompilerParams(vmem_limit_bytes=24 << 20),
        cost_estimate=QUICK,
    )(mine, theirs, weight, bias, cotangent)


def finish_kernel(*refs):
    mine, theirs = refs[:2]
    parts, (out, weight_grad, bias_grad) = refs[2:-3], refs[-3:]
    for n in range(parts[0].shape[0]):
        total = parts[0][n].astype(jnp.float32)
        for part in parts[1:]:
            total = total + part[n].astype(jnp.float32)
        out[n * BS : (n + 1) * BS] = total.T
    grads = mine[...].astype(jnp.float32) + theirs[...].astype(jnp.float32)
    channels = weight_grad.shape[0]
    weight_grad[...] = grads[:channels]
    bias_grad[...] = grads[channels : channels + 1]


def finish(parts, mine, theirs):
    per, channels, nodes = parts[0].shape
    units = mine.shape[1]
    out_shape = [
        jax.ShapeDtypeStruct(shape, jnp.float32)
        for shape in ((per * nodes, channels), (channels, units), (1, units))
    ]
    return pl.pallas_call(
        finish_kernel,
        out_shape=out_shape,
        in_specs=[VMEM] * (len(parts) + 2),
        out_specs=[VMEM] * 3,
        compiler_params=pltpu.CompilerParams(vmem_limit_bytes=16 << 20),
        cost_estimate=QUICK,
    )(mine, theirs, *parts)


def on_device(
    features, weight, bias_terms, blocks, block_rows, block_cols, tile_slot_count, cotangent
):
    own_rows, channels = features.shape
    row_devices, col_devices = lax.axis_size("row"), lax.axis_size("col")
    per = own_rows // BS
    row_blocks, column_blocks = per * col_devices, per * row_devices
    inner = inner_of(row_devices)
    on_col = tree(col_devices // 2, 2)
    across = col_devices - 2
    on_col = [route for route in on_col if route[0] != across]

    outer_steps = [inner * mask for mask in mirror_masks(row_devices // inner)]
    inner_steps = mirror_masks(inner)
    there = list(zip(outer_steps + inner_steps, outer_steps[:-1] + inner_steps + outer_steps[-1:]))
    back_steps = [(mask, mask) for mask in outer_steps + inner_steps]
    count = len(there)
    assert 1 << count == row_devices
    codes = sorted(range(1, row_devices), key=lambda code: (code.bit_count(), code))
    late_codes = codes[-(row_devices // 4) :]
    first_codes = codes[-1:]
    late_columns = [offset_of(code, there) for code in late_codes]
    first = [offset_of(code, back_steps) for code in first_codes]
    bits = widths(blocks.shape[0], row_blocks, column_blocks)
    indices = jnp.concatenate([block_rows, block_cols, tile_slot_count], axis=0)[:, 0]
    table, held = prep(indices, blocks, per, bits, late_columns, first)
    pieces = {0: features.reshape(per, BS, channels)}
    queue = Queue()
    for code in codes:
        parent, step = last_step(code)
        pieces[code] = row_swap(queue.tie(pieces[parent]), there[step], f"features_{code}")
        if code == 1:
            pieces[code] = after(pieces[code], table)
        if code == 1 << len(outer_steps) - 1:
            other_cotangent = swap(queue.tie(cotangent), "col", across, "cotangent")
    early = {offset_of(c, there): p for c, p in pieces.items() if c not in late_codes}
    late = {offset_of(c, there): p for c, p in pieces.items() if c in late_codes}
    total = sparse(FORWARD_EARLY, bits, table, held, early, "row", "col", column_blocks, row_blocks)
    sums = sparse(
        FORWARD_LATE, bits, table, held, late, "row", "col", column_blocks, row_blocks, total,
        {(d, d): jnp.float32 if d in (0, across) else jnp.bfloat16 for d in range(col_devices)}, per,
    )

    terms = collect(dict(enumerate(sums)), "col", on_col)
    terms[0][0] = after(terms[0][0], other_cotangent)
    mine = add(terms[0]).astype(jnp.bfloat16)
    others = add(terms[across]).astype(jnp.bfloat16)
    to_mine, to_others = swap(others, "col", across), swap(mine, "col", across)
    scaling = 1.0 / math.sqrt(own_rows * row_devices * col_devices)
    bias = bias_terms.reshape(1, -1)
    hidden, back, grads = dense(mine, to_mine, weight, bias, cotangent, scaling, True)
    other_back, other_grads = dense(
        others, to_others, weight, bias, other_cotangent, scaling, False
    )
    grads = grads + other_grads
    grads = grads + swap(grads, "col", 1)
    for mask in mirror_masks(col_devices // 2)[1:]:
        grads = grads + swap(grads, "col", 2 * mask)

    rows = spread({0: back, across: other_back}, "col", on_col)
    types = {code: jnp.bfloat16 if code else jnp.float32 for code in range(row_devices)}
    rest = [code for code in range(row_devices) if code not in first_codes]
    rows = {(d, d): p for d, p in rows.items()}
    leave_first, leave_last = [
        sparse(
            which, bits, table, held, rows, "col", "row", row_blocks, column_blocks,
            None, {offset_of(c, back_steps): types[c] for c in chosen}, per,
        )
        for which, chosen in ((BACK_FIRST, first_codes), (BACK_LAST, rest))
    ]
    sums = dict(zip(first_codes, leave_first)) | dict(zip(rest, leave_last))
    whole_way = [(1 << n) - 1 for n in range(1, count + 1)]
    outer_codes = (1 << len(outer_steps)) - 1
    stages = {code: code.bit_count() + (code & outer_codes == 0) for code in codes}
    order = sorted(
        codes, key=lambda code: (-stages[code], code != 1 + (1 << count - 1), code not in whole_way, -code)
    )
    grad_steps = list(range(count - 2, -1, -1)) + [count - 1]
    terms = {code: [p] for code, p in sums.items()}
    queue = Queue()
    mine, theirs = grads.astype(jnp.bfloat16), None
    for n, code in enumerate(order):
        parent, step = last_step(code)
        total = add(terms.pop(code)).astype(jnp.bfloat16)
        terms[parent].append(row_swap(queue.tie(total), back_steps[step], f"sums_{code}"))
        ends = n + 1 == len(order)
        if not ends and stages[order[n + 1]] == stages[code]:
            continue
        for step in grad_steps if ends else grad_steps[:1]:
            if theirs is not None:
                mine = add([mine, after(theirs, queue.last)]).astype(jnp.bfloat16)
            theirs = row_swap(queue.tie(mine), back_steps[step], f"gradients_{step}")
        grad_steps = grad_steps[1:]
    feat_grad, weight_grad, bias_grad = finish(terms[0], mine, theirs)
    return hidden, feat_grad, weight_grad, bias_grad.reshape(-1)


def solution(mesh):
    return jax.shard_map(
        on_device,
        mesh=mesh,
        in_specs=(
            P(("col", "row"), None),
            P(),
            P(),
            P("row", "col", None),
            P("row", "col"),
            P("row", "col"),
            P("row", "col"),
            P(("row", "col"), None),
        ),
        out_specs=(P(("row", "col"), None), P(("col", "row"), None), P(), P()),
        check_vma=False,
    )
```
